512 devices in a mesh: col: 64 (over z, x), wa: 8 (over y, core).
Axes of the slice: x: 4, y: 4, z: 16, core: 2. Of those that a mesh axis runs over, the one named last changes fastest.
Arguments:
- visibilities: bfloat16 [64, 8, 64, 2, 128], P('col', 'wa'), may hold values from -6 to 6
- visibility_uv_offsets: bfloat16 [64, 8, 64, 2, 128], P('col', 'wa'), may hold values from -16 to 16
- block_owner_index: int32 [64, 8, 64, 1], P('col', 'wa'), may hold values from 0 to 63; in each aligned block of 64 rows (0 to 63, 64 to 127, ..., all dimensions but the last counted through in order) at most 2 rows name the same one
- block_cell_number: int32 [64, 8, 64], P('col', 'wa'), may hold values from 0 to 1023
- live_counts: int32 [64, 8], P('col', 'wa'), may hold values from 48 to 64, as said below
- touch_lists: int32 [128, 12], P('col'), may hold values from -1 to 15, as said below
Outputs:
- facets: float32 [1024, 128], P(('col', 'wa'))
The draws below stay inside these ranges and needn't reach their ends.
Inputs may be any that keep to these rules, and one draw needn't show every extreme that they name: `block_owner_index`: on every device at most 2 of its 64 block slots, live or not, name one owner; on some device one owner is named exactly 2 times. `live_counts`: the live slots of a device are its first ones; some device has all 64 live. `touch_lists`: row c names 6 to 12 different facets in its first places and -1 in the rest; some row names 12 facets.
All inputs are finite; a program needn't handle non-finite values.
Results may differ from the reference program's by a relative error of at most 0.0036.
Values may be sent and summed in bfloat16 or wider, within the bound.
No kernel may reach another device: no remote copies, remote signals or barrier semaphores. Data moves between devices by JAX's collectives and lax.ppermute only.
A program may use at most 64 MiB of HBM per device.

```python
import math
import jax
import jax.numpy as jnp
import numpy as np
from jax import lax

S = 64
BLOCK_VISIBILITY = 128
RANGE_PLANES = 16
FACETS = 16
TOUCH = 12
DEVICE_COLUMNS = 2
COLUMN_SUBGRIDS = 32
DEVICE_SLOTS = 64
OWNER_SLOT_LIMIT = 2
N_COL = 64
N_WA = 8


def draw_live_counts(key, part):
    key = jax.random.fold_in(key, 11)
    leading_key, second_key, third_key = jax.random.split(key, 3)
    device_count_total = N_COL * N_WA
    smallest_count = DEVICE_SLOTS * 3 // 4
    slot_counts = jax.random.randint(leading_key, (device_count_total,), smallest_count, DEVICE_SLOTS + 1)
    most_filled = jax.random.randint(second_key, (), 0, device_count_total)
    least_filled = (most_filled + 1 + jax.random.randint(third_key, (), 0, device_count_total - 1)) % device_count_total
    slot_counts = slot_counts.at[most_filled].set(DEVICE_SLOTS).at[least_filled].set(smallest_count)
    return slot_counts.reshape(N_COL, N_WA).astype(jnp.int32)


def draw_touch_lists(key, part):
    key = jax.random.fold_in(key, 23)
    order_key, count_key, full_key = jax.random.split(key, 3)
    column_total = DEVICE_COLUMNS * N_COL
    column_keys = jax.random.split(order_key, column_total)
    orders = jax.vmap(lambda column_key: jax.random.permutation(column_key, FACETS))(column_keys)[:, :TOUCH]
    slot_counts = jax.random.randint(count_key, (column_total,), TOUCH // 2, TOUCH + 1)
    slot_counts = slot_counts.at[jax.random.randint(full_key, (), 0, column_total)].set(TOUCH)
    places = jnp.arange(TOUCH)
    return jnp.where(places[None, :] < slot_counts[:, None], orders, -1).astype(jnp.int32)


def plant(entries, own_key, smallest, top_value):
    spot = [jax.random.randint(jax.random.fold_in(own_key, axis), (), 0, length) for axis, length in enumerate(entries.shape)]
    longest = entries.shape.index(max(entries.shape))
    neighbour = spot[:longest] + [(spot[longest] + 1) % entries.shape[longest]] + spot[longest + 1:]
    return entries.at[tuple(spot)].set(smallest).at[tuple(neighbour)].set(top_value)


def shard_levels(rng, dims, cuts, smallest, high):
    factor_of = 1.0
    for dim, shards_of in cuts:
        draws = jax.random.uniform(jax.random.fold_in(jax.random.fold_in(rng, 6), dim), (shards_of,), jnp.float32, smallest / len(cuts), high / len(cuts))
        factor_of = factor_of * jnp.repeat(jnp.exp(draws), dims[dim] // shards_of).reshape((-1,) + (1,) * (len(dims) - 1 - dim))
    return factor_of


def routed_block(key, own, number, rows, number_of, top, reach, skew):
    order = jax.random.permutation(key, number_of)
    packed, usual = portions_of(number_of, rows * top, reach, skew, True), portions_of(number_of, rows * top, reach, skew, False)
    places = jnp.arange(number_of)

    def named(sizes, rotation):
        used = int((sizes > 0).sum())
        fixed = max(1, used // 4)
        moved = fixed + (places - fixed + rotation * (used - fixed)) % max(1, number_of - fixed)
        return jnp.zeros((number_of,), jnp.int32).at[order[jnp.where(places < fixed, places, moved)]].set(jnp.asarray(sizes, jnp.int32))

    sizes = jnp.where(number % 4 == 0, named(packed, number // 4), named(usual, number - number // 4 - 1))
    mixed = jax.random.permutation(jax.random.fold_in(own, 3), number_of)
    donor, taker = mixed[0:number_of // 2 * 2:2], mixed[1:number_of // 2 * 2:2]
    room = jnp.minimum(sizes[donor] - 1, reach - sizes[taker]) // 2
    room = jnp.where((donor == order[0]) | (taker == order[0]) | (sizes[taker] == 0), 0, jnp.maximum(room, 0))
    moved = jax.random.randint(jax.random.fold_in(own, 4), (number_of // 2,), 0, 1 << 20) % (room + 1)
    sizes = sizes.at[donor].add(-moved).at[taker].add(moved)
    items = jnp.searchsorted(jnp.cumsum(sizes), jnp.arange(rows * top), side="right").astype(jnp.int32)
    grid = items.reshape(top, rows).T
    grid = grid[jax.random.permutation(jax.random.fold_in(own, 1), rows)]
    rotation = jax.random.randint(jax.random.fold_in(own, 2), (rows, 1), 0, top)
    return jnp.take_along_axis(grid, (jnp.arange(top)[None, :] + rotation) % top, axis=1)


def portions_of(amount, total, bound, lean, full):
    loads = [(1 << 20) // math.isqrt(standing ** lean) + 1 for standing in range(1, amount + 1)]
    largest = bound if full else min(bound, max(-(-total // amount), total * loads[0] // sum(loads)))
    least = 1 if total - largest >= amount - 1 else 0
    given, surplus = [largest] + [least] * (amount - 1), total - largest - least * (amount - 1)
    while surplus > 0:
        candidates = [i for i in range(1, amount) if given[i] < largest] or [i for i in range(1, amount) if given[i] < bound]
        mass, budget = sum([loads[i] for i in candidates]), surplus
        for i in candidates:
            addition = min(bound - given[i], max(1, budget * loads[i] // mass), surplus)
            given[i] = given[i] + addition
            surplus = surplus - addition
    return np.array(given)


def noise(own_key, shape, width, limit, shards=(), held_as=jnp.bfloat16):
    result = width * jax.random.normal(own_key, shape, jnp.float32)
    if shards:
        result = result * shard_levels(own_key, shape, shards, -0.22, 0.18)
    return jnp.clip(result, -limit, limit).astype(held_as)


def setup_inputs(seed: int = 0) -> dict:
    arg_keys = jax.random.split(jax.random.key(seed), 7)
    visibilities = noise(arg_keys[0], (N_COL, N_WA, DEVICE_SLOTS, 2, BLOCK_VISIBILITY), 1.0, 6.0, ((0, 64), (1, 8)))
    visibility_uv_offsets = jnp.clip(jax.random.uniform(arg_keys[1], (N_COL, N_WA, DEVICE_SLOTS, 2, BLOCK_VISIBILITY), jnp.float32, -16.0, 16.0) * shard_levels(arg_keys[1], (N_COL, N_WA, DEVICE_SLOTS, 2, BLOCK_VISIBILITY), ((0, 64), (1, 8)), -0.4, 0.0), -16.0, 16.0).astype(jnp.bfloat16)
    block_owner_index_keys = jax.random.split(jax.random.fold_in(arg_keys[2], 1), N_COL * N_WA * DEVICE_SLOTS // DEVICE_SLOTS)
    block_owner_index_turns = jax.random.permutation(jax.random.fold_in(arg_keys[2], 3), N_COL * N_WA * DEVICE_SLOTS // DEVICE_SLOTS)
    block_owner_index = jax.vmap(lambda own, number: routed_block(jax.random.fold_in(arg_keys[2], 2), own, number, DEVICE_SLOTS, N_COL, 1, OWNER_SLOT_LIMIT, 2))(block_owner_index_keys, block_owner_index_turns).reshape((N_COL, N_WA, DEVICE_SLOTS, 1))
    block_cell_number = plant(jax.random.randint(arg_keys[3], (N_COL, N_WA, DEVICE_SLOTS), 0, DEVICE_COLUMNS * COLUMN_SUBGRIDS * RANGE_PLANES), jax.random.fold_in(arg_keys[3], 1), 0, (DEVICE_COLUMNS * COLUMN_SUBGRIDS * RANGE_PLANES) - 1).astype(jnp.int32)
    live_counts = draw_live_counts(jax.random.fold_in(arg_keys[6], 71), 0)
    touch_lists = draw_touch_lists(jax.random.fold_in(arg_keys[6], 71), 0)
    return dict(visibilities=visibilities, visibility_uv_offsets=visibility_uv_offsets, block_owner_index=block_owner_index, block_cell_number=block_cell_number, live_counts=live_counts, touch_lists=touch_lists)


FULL_TURN = 2.0 * math.pi
FIELD_WIDTH = 0.2
CELL_STEP = 0.37
WTERM_LIMIT = 4000.0
HIGHEST = lax.Precision.HIGHEST

def pixel_offsets(length):
    return jnp.arange(length).astype(jnp.float32) - jnp.float32(length // 2)

def phase_lag(length):
    direction = pixel_offsets(length) * (FIELD_WIDTH / length)
    radius = direction[:, None] ** 2 + direction[None, :] ** 2
    return -radius / (1.0 + jnp.sqrt(1.0 - radius))

def phasor_tables(coords, values):
    offsets = pixel_offsets(S) * (FULL_TURN / S)
    angle_u = coords[:, 0, :, None] * offsets
    angle_v = coords[:, 1, :, None] * offsets
    cosine_v = jnp.cos(angle_v)
    sine_v = jnp.sin(angle_v)
    real_part = values[:, 0, :, None]
    imag_part = values[:, 1, :, None]
    weighted_real = (real_part * cosine_v - imag_part * sine_v).astype(jnp.bfloat16)
    weighted_imag = (real_part * sine_v + imag_part * cosine_v).astype(jnp.bfloat16)
    left_table = jnp.concatenate([jnp.cos(angle_u).astype(jnp.bfloat16), jnp.sin(angle_u).astype(jnp.bfloat16)], axis=1)
    upper_rows = jnp.concatenate([weighted_real, weighted_imag], axis=2)
    lower_rows = jnp.concatenate([-weighted_imag, weighted_real], axis=2)
    right_table = jnp.concatenate([upper_rows, lower_rows], axis=1)
    return (left_table, right_table)

def complex_times(operand, factor_real, factor_imag, extent):
    operand_real = operand[..., :extent]
    operand_imag = operand[..., extent:]
    return jnp.concatenate([operand_real * factor_real - operand_imag * factor_imag, operand_real * factor_imag + operand_imag * factor_real], axis=-1)

def shift_matrices(shifts):
    frequency = pixel_offsets(S) * (FULL_TURN / S)
    position = jnp.arange(S).astype(jnp.float32)
    left_angle = position[:, None] * frequency[None, :]
    right_angle = (position[None, :] + shifts[:, None])[..., None] * frequency
    cos_left = jnp.cos(left_angle)
    sin_left = jnp.sin(left_angle)
    cos_right = jnp.cos(right_angle)
    sin_right = jnp.sin(right_angle)
    real_part = jnp.einsum('xk,flk->fxl', cos_left, cos_right, precision=HIGHEST) + jnp.einsum('xk,flk->fxl', sin_left, sin_right, precision=HIGHEST)
    imag_part = jnp.einsum('xk,flk->fxl', sin_left, cos_right, precision=HIGHEST) - jnp.einsum('xk,flk->fxl', cos_left, sin_right, precision=HIGHEST)
    return (real_part / S, imag_part / S)

def facet_geometry():
    facet_ids = jnp.arange(FACETS)
    facet_column = (facet_ids % 4).astype(jnp.float32)
    facet_row = (facet_ids // 4).astype(jnp.float32)
    return (facet_column, facet_row)

def facet_weights(column_ids, row_ids, touched, column_total):
    facet_column, facet_row = facet_geometry()
    column_phase = FULL_TURN * CELL_STEP * (column_ids - column_total / 2 + 0.5)[:, None] * ((facet_column - 1.5) / 4)[None, :]
    row_phase = FULL_TURN * CELL_STEP * (row_ids - COLUMN_SUBGRIDS / 2 + 0.5)[:, None] * ((facet_row - 1.5) / 4)[None, :]
    angle_all = column_phase[:, None, :] + row_phase[None, :, :]
    return (jnp.cos(angle_all) * touched[:, None, :], jnp.sin(angle_all) * touched[:, None, :])

def combine_towers(weight_real, weight_imag, towers):
    swapped = jnp.concatenate([-towers[..., S:], towers[..., :S]], axis=-1)
    first_sum = jnp.einsum('cjf,cjlq->flq', weight_real, towers, precision=HIGHEST)
    second_sum = jnp.einsum('cjf,cjlq->flq', weight_imag, swapped, precision=HIGHEST)
    return first_sum + second_sum

def facet_image(summed):
    facet_column, facet_row = facet_geometry()
    shift_real, shift_imag = shift_matrices((facet_column + 0.5) / 4)
    other_real, other_imag = shift_matrices((facet_row + 0.5) / 4)
    swapped = jnp.concatenate([-summed[..., S:], summed[..., :S]], axis=-1)
    rotated = jnp.einsum('fxl,flq->fxq', shift_real, summed, precision=HIGHEST) + jnp.einsum('fxl,flq->fxq', shift_imag, swapped, precision=HIGHEST)
    rotated_real = rotated[..., :S]
    rotated_imag = rotated[..., S:]
    result_real = jnp.einsum('fxm,fym->fxy', rotated_real, other_real, precision=HIGHEST) - jnp.einsum('fxm,fym->fxy', rotated_imag, other_imag, precision=HIGHEST)
    result_imag = jnp.einsum('fxm,fym->fxy', rotated_real, other_imag, precision=HIGHEST) + jnp.einsum('fxm,fym->fxy', rotated_imag, other_real, precision=HIGHEST)
    return jnp.concatenate([result_real, result_imag], axis=-1)

def reference(visibilities, visibility_uv_offsets, block_owner_index, block_cell_number, live_counts, touch_lists):
    device_count_total = N_COL * N_WA
    column_total = DEVICE_COLUMNS * N_COL
    block_slot_index = jnp.arange(DEVICE_SLOTS).astype(jnp.int32)
    active_mask = (block_slot_index[None, :] < live_counts.reshape(device_count_total, 1)).astype(jnp.float32)
    owner_indices = block_owner_index.reshape(device_count_total, DEVICE_SLOTS)
    cell_numbers = block_cell_number.reshape(device_count_total, DEVICE_SLOTS)
    columns = owner_indices * DEVICE_COLUMNS + cell_numbers // (COLUMN_SUBGRIDS * RANGE_PLANES)
    target_indices = (columns * COLUMN_SUBGRIDS + cell_numbers // RANGE_PLANES % COLUMN_SUBGRIDS).astype(jnp.int32)
    planes = cell_numbers % RANGE_PLANES
    ranges = (jnp.arange(device_count_total) % N_WA).astype(jnp.int32)
    plane_step = 2.0 * WTERM_LIMIT / (RANGE_PLANES * N_WA)
    plane_depths = -WTERM_LIMIT + ((ranges[:, None] * RANGE_PLANES + planes).astype(jnp.float32) + 0.5) * plane_step
    lag_field = phase_lag(S)

    def accumulate(towers, block_entries):
        values, coords, target_rows, depth_row, live_row = block_entries
        left_table, right_table = phasor_tables(coords.astype(jnp.float32), values.astype(jnp.float32))
        block_grids = jnp.einsum('nkl,nkq->nlq', left_table.astype(jnp.float32), right_table.astype(jnp.float32), precision=HIGHEST)
        screen_angle = FULL_TURN * depth_row[:, None, None] * lag_field
        contrib = complex_times(block_grids, jnp.cos(screen_angle), jnp.sin(screen_angle), S) * live_row[:, None, None]
        return (towers.at[target_rows].add(contrib), None)
    towers = jnp.zeros((column_total * COLUMN_SUBGRIDS, S, 2 * S), jnp.float32)
    block_entries = (visibilities.reshape(device_count_total, DEVICE_SLOTS, 2, BLOCK_VISIBILITY), visibility_uv_offsets.reshape(device_count_total, DEVICE_SLOTS, 2, BLOCK_VISIBILITY), target_indices, plane_depths, active_mask)
    towers, unused = lax.scan(accumulate, towers, block_entries)
    towers = towers.reshape(column_total, COLUMN_SUBGRIDS, S, 2 * S)
    facet_ids = jnp.arange(FACETS)
    touched = jnp.any(touch_lists[:, :, None] == facet_ids[None, None, :], axis=1).astype(jnp.float32)
    column_ids = jnp.arange(column_total).astype(jnp.float32)
    row_ids = jnp.arange(COLUMN_SUBGRIDS).astype(jnp.float32)
    weight_real, weight_imag = facet_weights(column_ids, row_ids, touched, column_total)
    summed = combine_towers(weight_real, weight_imag, towers)
    scale_multiplier = 1.0 / math.sqrt(BLOCK_VISIBILITY * N_COL * N_WA * DEVICE_SLOTS)
    facet_field = facet_image(summed) * scale_multiplier
    return facet_field.reshape(FACETS * S, 2 * S)
```

```python
import functools
import math

import jax
import jax.numpy as jnp
import numpy as np
from jax import lax
from jax.experimental import pallas as pl
from jax.experimental.pallas import tpu as pltpu
from jax.sharding import PartitionSpec as P

S = 64
BLOCK_VISIBILITY = 128
RANGE_PLANES = 16
FACETS = 16
TOUCH = 12
DEVICE_COLUMNS = 2
COLUMN_SUBGRIDS = 32
DEVICE_SLOTS = 64
N_COL = 64
N_WA = 8

FULL_TURN = 2.0 * math.pi
FIELD_WIDTH = 0.2
CELL_STEP = 0.37
WTERM_LIMIT = 4000.0
SCALE = 1.0 / math.sqrt(BLOCK_VISIBILITY * N_COL * N_WA * DEVICE_SLOTS)
UNROLL = 4

f32 = jnp.float32
bf16 = jnp.bfloat16


def half_turn_fits():
    nodes = np.cos(np.pi * (np.arange(400) + 0.5) / 400) * 0.125 + 0.125
    root = np.sqrt(nodes)
    sine = np.polynomial.chebyshev.Chebyshev.fit(nodes, np.sin(np.pi * root) / root, 4, domain=[0, 0.25])
    cosine = np.polynomial.chebyshev.Chebyshev.fit(nodes, np.cos(np.pi * root), 5, domain=[0, 0.25])
    return tuple(
        [float(c) for c in fit.convert(kind=np.polynomial.Polynomial).coef] for fit in (sine, cosine)
    )


SINE_FIT, COSINE_FIT = half_turn_fits()


def horner(fit, z):
    total = fit[-1]
    for c in fit[-2::-1]:
        total = total * z + c
    return total


def cos_sin_turns(turns):
    h = turns - jnp.floor(turns + 0.5)
    z = h * h
    sine = h * horner(SINE_FIT, z)
    cosine = horner(COSINE_FIT, z)
    return 1.0 - 2.0 * (sine * sine), 2.0 * (sine * cosine)


def grid_kernel(cells, first_plane, vis_ref, uv_ref, out_ref, vis_rows, uv_rows, screen_a, screen_b):
    vis_rows[...] = vis_ref[...].astype(f32)
    uv_rows[...] = uv_ref[...].astype(f32)

    lane = lax.broadcasted_iota(jnp.int32, (S, 2 * S), 1)
    a = (lax.broadcasted_iota(jnp.int32, (S, 2 * S), 0) - S // 2).astype(f32) * (FIELD_WIDTH / S)
    e = ((lane & (S - 1)) - S // 2).astype(f32) * (FIELD_WIDTH / S)
    radius = a * a + e * e
    lag = -radius / (1.0 + jnp.sqrt(1.0 - radius))
    sign = jnp.where(lane < S, -1.0, 1.0).astype(f32)
    plane_step = 2.0 * WTERM_LIMIT / (RANGE_PLANES * N_WA)

    def make_screen(p, carry):
        depth = -WTERM_LIMIT + ((first_plane[0] + p).astype(f32) + 0.5) * plane_step
        cosine, sine = cos_sin_turns(depth * lag)
        screen_a[p] = cosine
        screen_b[p] = sine * sign
        return carry

    lax.fori_loop(0, RANGE_PLANES, make_screen, 0)

    fine = lax.broadcasted_iota(jnp.int32, (8, 1), 0).astype(f32) * (1.0 / S)
    coarse = (lax.broadcasted_iota(jnp.int32, (8, 1), 0) - 4).astype(f32) * (8.0 / S)

    def one_block(b):
        u = uv_rows[pl.ds(2 * b, 1), :]
        v = uv_rows[pl.ds(2 * b + 1, 1), :]
        vr = vis_rows[pl.ds(2 * b, 1), :]
        vi = vis_rows[pl.ds(2 * b + 1, 1), :]
        turns = jnp.concatenate([u * fine, u * coarse, v * fine, v * coarse], axis=0)
        c, s = cos_sin_turns(turns)
        cu, su, cua, sua = c[0:8], s[0:8], c[8:16], s[8:16]
        cv, sv, cva, sva = c[16:24], s[16:24], c[24:32], s[24:32]
        wra = vr * cva - vi * sva
        wia = vr * sva + vi * cva
        uc, us, wr, wi = [], [], [], []
        for k in range(8):
            ck, sk = cua[k : k + 1], sua[k : k + 1]
            uc.append(ck * cu - sk * su)
            us.append(sk * cu + ck * su)
            rk, ik = wra[k : k + 1], wia[k : k + 1]
            wr.append(rk * cv - ik * sv)
            wi.append(rk * sv + ik * cv)
        uc, us, wr, wi = [jnp.concatenate(t, axis=0).astype(bf16) for t in (uc, us, wr, wi)]
        left = jnp.concatenate([uc, us], axis=1)
        right = jnp.concatenate(
            [jnp.concatenate([wr, -wi], axis=1), jnp.concatenate([wi, wr], axis=1)], axis=0
        )
        grid = lax.dot_general(
            left, right, (((1,), (1,)), ((), ())), preferred_element_type=f32
        )
        plane = cells[b] & (RANGE_PLANES - 1)
        towers = grid * screen_a[plane] + pltpu.roll(grid, S, 1) * screen_b[plane]
        out_ref[pl.ds(b, S, stride=DEVICE_SLOTS), :] = towers

    def some_blocks(i, carry):
        for k in range(UNROLL):
            one_block(i * UNROLL + k)
        return carry

    lax.fori_loop(0, DEVICE_SLOTS // UNROLL, some_blocks, 0)


def split_bf16(x):
    high = x.astype(bf16)
    return high, (x - high.astype(f32)).astype(bf16)


def facet_kernel(live, owner_ref, cell_ref, touch_ref, shift_ref, towers_ref, out_ref, facet_ref):
    cell = cell_ref[...]
    column = owner_ref[...] * DEVICE_COLUMNS + cell // (COLUMN_SUBGRIDS * RANGE_PLANES)
    row = (cell // RANGE_PLANES) % COLUMN_SUBGRIDS
    facet = lax.broadcasted_iota(jnp.int32, (FACETS, 1), 0)
    fx = (facet % 4).astype(f32)
    fy = (facet // 4).astype(f32)
    columns = DEVICE_COLUMNS * N_COL
    turns = CELL_STEP * (
        (column.astype(f32) - columns / 2 + 0.5) * ((fx - 1.5) / 4)
        + (row.astype(f32) - COLUMN_SUBGRIDS / 2 + 0.5) * ((fy - 1.5) / 4)
    )
    cosine, sine = cos_sin_turns(turns)
    named = touch_ref[...]
    facet_lane = lax.broadcasted_iota(jnp.int32, (columns, FACETS), 1)
    touched = named[:, 0:1] == facet_lane
    for t in range(1, TOUCH):
        touched = touched | (named[:, t : t + 1] == facet_lane)
    touched = jnp.where(touched, 1.0, 0.0).astype(bf16)
    chosen = lax.broadcasted_iota(jnp.int32, (columns, DEVICE_SLOTS), 0) == column
    alive = lax.broadcasted_iota(jnp.int32, (columns, DEVICE_SLOTS), 1) < live[0]
    chosen = jnp.where(chosen & alive, 1.0, 0.0).astype(bf16)
    mask = lax.dot_general(touched, chosen, (((0,), (0,)), ((), ())), preferred_element_type=f32)
    weights = jnp.concatenate([cosine * mask, sine * mask], axis=0)
    high, low = split_bf16(weights)
    left = jnp.concatenate(
        [jnp.concatenate([high, high], axis=1), jnp.concatenate([low, jnp.zeros_like(low)], axis=1)],
        axis=0,
    )
    sign = jnp.where(lax.broadcasted_iota(jnp.int32, (FACETS, 2 * S), 1) < S, -1.0, 1.0).astype(f32)

    for l in range(0, S, 2):
        pair = jnp.concatenate(
            [
                towers_ref[l * DEVICE_SLOTS : (l + 1) * DEVICE_SLOTS, :],
                towers_ref[(l + 1) * DEVICE_SLOTS : (l + 2) * DEVICE_SLOTS, :],
            ],
            axis=1,
        )
        high, low = split_bf16(pair)
        sums = jnp.dot(left, jnp.concatenate([high, low], axis=0), preferred_element_type=f32)
        sums = sums[: 2 * FACETS] + sums[2 * FACETS :]
        for k in range(2):
            part = sums[:, 2 * S * k : 2 * S * (k + 1)]
            facet_ref[pl.ds(l + k, FACETS, stride=S), :] = (
                part[:FACETS] + sign * pltpu.roll(part[FACETS:], S, 1)
            )

    wide = jnp.where(lax.broadcasted_iota(jnp.int32, (S, 2 * S), 1) < S, -1.0, 1.0).astype(f32)
    for fx in range(4):
        plain = [facet_ref[(fx + 4 * fy) * S : (fx + 4 * fy + 1) * S, :] for fy in range(4)]
        turned = [wide * pltpu.roll(g, S, 1) for g in plain]
        stack = jnp.concatenate(
            [jnp.concatenate(plain, axis=1), jnp.concatenate(turned, axis=1)], axis=0
        )
        high, low = split_bf16(stack)
        shift = shift_ref[fx]
        first = jnp.dot(shift, high, preferred_element_type=f32)
        second = jnp.dot(shift[:S], low, preferred_element_type=f32)
        image = (first[:S] + first[S:] + second).reshape(N_WA, S // N_WA, 8 * S)
        rows = jnp.concatenate(
            [image[:, :, 2 * S * fy : 2 * S * (fy + 1)] for fy in range(4)], axis=1
        )
        out_ref[:, fx * 32 : (fx + 1) * 32, :] = rows.astype(out_ref.dtype)


def shift_matrix(d):
    k = np.arange(S) - S // 2
    x = np.arange(S)
    return np.exp(2j * np.pi * k * x[:, None] / S) @ np.exp(-2j * np.pi * k[:, None] * (x + d) / S) / S


def left_shifts():
    order = np.array([16 * q + 2 * w + i for w in range(N_WA) for q in range(4) for i in range(2)])
    tables = []
    for fx in range(4):
        shift = shift_matrix((fx + 0.5) / 4)[order] * SCALE
        table = np.concatenate([shift.real, shift.imag], axis=1).astype(np.float32)
        high = table.astype(jnp.bfloat16)
        low = (table - high.astype(np.float32)).astype(jnp.bfloat16)
        tables.append(np.concatenate([high, low], axis=0))
    return np.stack(tables)


def right_shifts():
    tables = []
    for fy in range(4):
        shift = shift_matrix((fy + 0.5) / 4).T
        tables.append(
            np.concatenate(
                [
                    np.concatenate([shift.real, shift.imag], axis=1),
                    np.concatenate([-shift.imag, shift.real], axis=1),
                ],
                axis=0,
            )
        )
    return np.stack(tables).astype(np.float32)


def middle_kernel(in_ref, out_ref):
    total = in_ref[0].astype(f32)
    for k in range(1, N_WA):
        total = total + in_ref[k].astype(f32)
    for fy in range(4):
        for fx in range(4):
            out_ref[(4 * fy + fx) * 8 : (4 * fy + fx + 1) * 8, :] = total[
                fx * 32 + fy * 8 : fx * 32 + fy * 8 + 8
            ]


def last_kernel(facet_row, in_ref, shift_ref, out_ref):
    total = in_ref[0]
    for k in range(1, N_COL):
        total = total + in_ref[k]
    rows = jnp.concatenate([total, jnp.zeros((6, 2 * S), f32)], axis=0)
    image = jnp.dot(rows, shift_ref[facet_row[0]], precision=lax.Precision.HIGHEST, preferred_element_type=f32)
    out_ref[...] = image[:2]


VMEM = pl.BlockSpec(memory_space=pltpu.VMEM)
SMEM = pl.BlockSpec(memory_space=pltpu.SMEM)


def shards(
    visibilities,
    visibility_uv_offsets,
    block_owner_index,
    block_cell_number,
    live_counts,
    touch_lists,
):
    col_index = lax.axis_index("col")
    range_index = lax.axis_index("wa")
    named = lax.all_to_all(
        jnp.broadcast_to(touch_lists[None], (N_COL, DEVICE_COLUMNS, TOUCH)),
        "col",
        split_axis=0,
        concat_axis=0,
        tiled=True,
    ).reshape(N_COL * DEVICE_COLUMNS, TOUCH)
    cells = block_cell_number.reshape(DEVICE_SLOTS)
    towers = pl.pallas_call(
        grid_kernel,
        out_shape=jax.ShapeDtypeStruct((S * DEVICE_SLOTS, 2 * S), f32),
        in_specs=[SMEM, SMEM, VMEM, VMEM],
        out_specs=VMEM,
        scratch_shapes=[
            pltpu.VMEM((2 * DEVICE_SLOTS, BLOCK_VISIBILITY), f32),
            pltpu.VMEM((2 * DEVICE_SLOTS, BLOCK_VISIBILITY), f32),
            pltpu.VMEM((RANGE_PLANES, S, 2 * S), f32),
            pltpu.VMEM((RANGE_PLANES, S, 2 * S), f32),
        ],
        compiler_params=pltpu.CompilerParams(vmem_limit_bytes=24 * 1024 * 1024),
        cost_estimate=pl.CostEstimate(flops=300_000_000, bytes_accessed=2_200_000, transcendentals=0),
        name="grid_blocks",
    )(
        cells,
        (range_index * RANGE_PLANES).reshape(1).astype(jnp.int32),
        visibilities.reshape(2 * DEVICE_SLOTS, BLOCK_VISIBILITY),
        visibility_uv_offsets.reshape(2 * DEVICE_SLOTS, BLOCK_VISIBILITY),
    )
    partial_rows = pl.pallas_call(
        facet_kernel,
        out_shape=jax.ShapeDtypeStruct((N_WA, FACETS * S // N_WA, 2 * S), bf16),
        in_specs=[SMEM, VMEM, VMEM, VMEM, VMEM, VMEM],
        out_specs=VMEM,
        scratch_shapes=[pltpu.VMEM((FACETS * S, 2 * S), f32)],
        compiler_params=pltpu.CompilerParams(vmem_limit_bytes=24 * 1024 * 1024),
        name="facet_sums",
    )(
        live_counts.reshape(1),
        block_owner_index.reshape(1, DEVICE_SLOTS),
        block_cell_number.reshape(1, DEVICE_SLOTS),
        named,
        jnp.asarray(left_shifts()),
        towers,
    )
    arrived = lax.all_to_all(partial_rows, "wa", split_axis=0, concat_axis=0, tiled=True)
    range_rows = pl.pallas_call(
        middle_kernel,
        out_shape=jax.ShapeDtypeStruct((FACETS * S // N_WA, 2 * S), f32),
        in_specs=[VMEM],
        out_specs=VMEM,
        name="range_sums",
    )(arrived)
    arrived = lax.all_to_all(
        range_rows.reshape(N_COL, 2, 2 * S), "col", split_axis=0, concat_axis=0, tiled=True
    )
    return pl.pallas_call(
        last_kernel,
        out_shape=jax.ShapeDtypeStruct((2, 2 * S), f32),
        in_specs=[SMEM, VMEM, VMEM],
        out_specs=VMEM,
        name="column_sums",
    )((col_index // 16).reshape(1).astype(jnp.int32), arrived, jnp.asarray(right_shifts()))


def solution(mesh):
    placed = (
        P("col", "wa", None, None, None),
        P("col", "wa", None, None, None),
        P("col", "wa", None, None),
        P("col", "wa", None),
        P("col", "wa"),
        P("col", None),
    )
    return jax.shard_map(
        shards, mesh=mesh, in_specs=placed, out_specs=P(("col", "wa"), None), check_vma=False
    )
```

```python
import functools
import math

import jax
import jax.numpy as jnp
import numpy as np
from jax import lax
from jax.experimental import pallas as pl
from jax.experimental.pallas import tpu as pltpu
from jax.sharding import Mesh, PartitionSpec as P

S = 64
BLOCK_VISIBILITY = 128
RANGE_PLANES = 16
FACETS = 16
TOUCH = 12
DEVICE_COLUMNS = 2
COLUMN_SUBGRIDS = 32
DEVICE_SLOTS = 64
N_COL = 64
N_WA = 8

FULL_TURN = 2.0 * math.pi
FIELD_WIDTH = 0.2
CELL_STEP = 0.37
WTERM_LIMIT = 4000.0
SCALE = 1.0 / math.sqrt(BLOCK_VISIBILITY * N_COL * N_WA * DEVICE_SLOTS)
UNROLL = 4
GROUP = 32
TOUCH_Z, TOUCH_X = 10, 2
PLANE_X, PLANE_WA = 0, 0
LINE_Z = 8

f32 = jnp.float32
bf16 = jnp.bfloat16


def half_turn_fits():
    nodes = np.cos(np.pi * (np.arange(400) + 0.5) / 400) * 0.125 + 0.125
    root = np.sqrt(nodes)
    sine = np.polynomial.chebyshev.Chebyshev.fit(nodes, np.sin(np.pi * root) / root, 4, domain=[0, 0.25])
    cosine = np.polynomial.chebyshev.Chebyshev.fit(nodes, np.cos(np.pi * root), 5, domain=[0, 0.25])
    return tuple(
        [float(c) for c in fit.convert(kind=np.polynomial.Polynomial).coef] for fit in (sine, cosine)
    )


SINE_FIT, COSINE_FIT = half_turn_fits()


def horner(fit, z):
    total = fit[-1]
    for c in fit[-2::-1]:
        total = total * z + c
    return total


def cos_sin_turns(turns):
    h = turns - jnp.floor(turns + 0.5)
    z = h * h
    sine = h * horner(SINE_FIT, z)
    cosine = horner(COSINE_FIT, z)
    return 1.0 - 2.0 * (sine * sine), 2.0 * (sine * cosine)


def grid_kernel(
    first_plane,
    packed_ref,
    out_ref,
    cell_row,
    cells,
    vis_rows,
    uv_rows,
    screen_a,
    screen_b,
    arrival,
):
    cell_row[...] = packed_ref[4 * DEVICE_SLOTS : 4 * DEVICE_SLOTS + 8, :].astype(jnp.int32)
    copy = pltpu.make_async_copy(cell_row, cells, arrival)
    copy.start()
    vis_rows[...] = packed_ref[: 2 * DEVICE_SLOTS, :]
    uv_rows[...] = packed_ref[2 * DEVICE_SLOTS : 4 * DEVICE_SLOTS, :]

    lane = lax.broadcasted_iota(jnp.int32, (S, 2 * S), 1)
    a = (lax.broadcasted_iota(jnp.int32, (S, 2 * S), 0) - S // 2).astype(f32) * (FIELD_WIDTH / S)
    e = ((lane & (S - 1)) - S // 2).astype(f32) * (FIELD_WIDTH / S)
    radius = a * a + e * e
    lag = -radius / (1.0 + jnp.sqrt(1.0 - radius))
    sign = jnp.where(lane < S, -1.0, 1.0).astype(f32)
    plane_step = 2.0 * WTERM_LIMIT / (RANGE_PLANES * N_WA)

    def make_screen(p, carry):
        depth = -WTERM_LIMIT + ((first_plane[0] + p).astype(f32) + 0.5) * plane_step
        cosine, sine = cos_sin_turns(depth * lag)
        screen_a[p] = cosine
        screen_b[p] = sine * sign
        return carry

    lax.fori_loop(0, RANGE_PLANES, make_screen, 0)

    copy.wait()

    fine = lax.broadcasted_iota(jnp.int32, (8, 1), 0).astype(f32) * (1.0 / S)
    coarse = (lax.broadcasted_iota(jnp.int32, (8, 1), 0) - 4).astype(f32) * (8.0 / S)

    def one_block(b):
        u = uv_rows[pl.ds(2 * b, 1), :]
        v = uv_rows[pl.ds(2 * b + 1, 1), :]
        vr = vis_rows[pl.ds(2 * b, 1), :]
        vi = vis_rows[pl.ds(2 * b + 1, 1), :]
        turns = jnp.concatenate([u * fine, u * coarse, v * fine, v * coarse], axis=0)
        c, s = cos_sin_turns(turns)
        cu, su, cua, sua = c[0:8], s[0:8], c[8:16], s[8:16]
        cv, sv, cva, sva = c[16:24], s[16:24], c[24:32], s[24:32]
        wra = vr * cva - vi * sva
        wia = vr * sva + vi * cva
        uc, us, wr, wi = [], [], [], []
        for k in range(8):
            ck, sk = cua[k : k + 1], sua[k : k + 1]
            uc.append(ck * cu - sk * su)
            us.append(sk * cu + ck * su)
            rk, ik = wra[k : k + 1], wia[k : k + 1]
            wr.append(rk * cv - ik * sv)
            wi.append(rk * sv + ik * cv)
        uc, us, wr, wi = [jnp.concatenate(t, axis=0).astype(bf16) for t in (uc, us, wr, wi)]
        left = jnp.concatenate([uc, us], axis=1)
        right = jnp.concatenate(
            [jnp.concatenate([wr, -wi], axis=1), jnp.concatenate([wi, wr], axis=1)], axis=0
        )
        grid = lax.dot_general(
            left, right, (((1,), (1,)), ((), ())), preferred_element_type=f32
        )
        plane = cells[0, b] & (RANGE_PLANES - 1)
        towers = grid * screen_a[plane] + pltpu.roll(grid, S, 1) * screen_b[plane]
        out_ref[pl.ds(b, S, stride=DEVICE_SLOTS), :] = towers

    def some_blocks(i, carry):
        for k in range(UNROLL):
            one_block(i * UNROLL + k)
        return carry

    lax.fori_loop(0, DEVICE_SLOTS // UNROLL, some_blocks, 0)


def split_bf16(x):
    high = x.astype(bf16)
    return high, (x - high.astype(f32)).astype(bf16)


def facet_kernel(live, owner_ref, cell_ref, touch_ref, shift_ref, towers_ref, out_ref, facet_ref, rows_ref):
    cell = cell_ref[...]
    column = owner_ref[...] * DEVICE_COLUMNS + cell // (COLUMN_SUBGRIDS * RANGE_PLANES)
    row = (cell // RANGE_PLANES) % COLUMN_SUBGRIDS
    facet = lax.broadcasted_iota(jnp.int32, (FACETS, 1), 0)
    fx = (facet % 4).astype(f32)
    fy = (facet // 4).astype(f32)
    columns = DEVICE_COLUMNS * N_COL
    turns = CELL_STEP * (
        (column.astype(f32) - columns / 2 + 0.5) * ((fx - 1.5) / 4)
        + (row.astype(f32) - COLUMN_SUBGRIDS / 2 + 0.5) * ((fy - 1.5) / 4)
    )
    cosine, sine = cos_sin_turns(turns)
    named = touch_ref[...]
    facet_lane = lax.broadcasted_iota(jnp.int32, (columns, FACETS), 1)
    touched = named[:, 0:1] == facet_lane
    for t in range(1, TOUCH):
        touched = touched | (named[:, t : t + 1] == facet_lane)
    touched = jnp.where(touched, 1.0, 0.0).astype(bf16)
    owner = owner_ref[...]
    place = ((owner // 4 + 16 - TOUCH_Z) % 16) * 4 + (owner + 4 - TOUCH_X) % 4
    place = place * DEVICE_COLUMNS + cell // (COLUMN_SUBGRIDS * RANGE_PLANES)
    chosen = lax.broadcasted_iota(jnp.int32, (columns, DEVICE_SLOTS), 0) == place
    alive = lax.broadcasted_iota(jnp.int32, (columns, DEVICE_SLOTS), 1) < live[0]
    chosen = jnp.where(chosen & alive, 1.0, 0.0).astype(bf16)
    mask = lax.dot_general(touched, chosen, (((0,), (0,)), ((), ())), preferred_element_type=f32)
    weights = jnp.concatenate([cosine * mask, sine * mask], axis=0)
    high, low = split_bf16(weights)
    left = jnp.concatenate(
        [jnp.concatenate([high, high], axis=1), jnp.concatenate([low, jnp.zeros_like(low)], axis=1)],
        axis=0,
    )
    sign = jnp.where(lax.broadcasted_iota(jnp.int32, (FACETS, 2 * S), 1) < S, -1.0, 1.0).astype(f32)

    for l in range(0, S, 2):
        pair = jnp.concatenate(
            [
                towers_ref[l * DEVICE_SLOTS : (l + 1) * DEVICE_SLOTS, :],
                towers_ref[(l + 1) * DEVICE_SLOTS : (l + 2) * DEVICE_SLOTS, :],
            ],
            axis=1,
        )
        high, low = split_bf16(pair)
        sums = jnp.dot(left, jnp.concatenate([high, low], axis=0), preferred_element_type=f32)
        sums = sums[: 2 * FACETS] + sums[2 * FACETS :]
        for k in range(2):
            part = sums[:, 2 * S * k : 2 * S * (k + 1)]
            facet_ref[pl.ds(l + k, FACETS, stride=S), :] = (
                part[:FACETS] + sign * pltpu.roll(part[FACETS:], S, 1)
            )

    wide = jnp.where(lax.broadcasted_iota(jnp.int32, (S, 2 * S), 1) < S, -1.0, 1.0).astype(f32)
    for fx in range(4):
        plain = [facet_ref[(fx + 4 * fy) * S : (fx + 4 * fy + 1) * S, :] for fy in range(4)]
        turned = [wide * pltpu.roll(g, S, 1) for g in plain]
        stack = jnp.concatenate(
            [jnp.concatenate(plain, axis=1), jnp.concatenate(turned, axis=1)], axis=0
        )
        high, low = split_bf16(stack)
        shift = shift_ref[fx]
        first = jnp.dot(shift, high, preferred_element_type=f32)
        second = jnp.dot(shift[:S], low, preferred_element_type=f32)
        image = first[:S] + first[S:] + second
        for fy in range(4):
            place = (fx + 4 * fy - LINE_Z) % FACETS
            for i in range(2):
                rows_ref[pl.ds(2 * place + i, GROUP, stride=GROUP), :] = image[
                    GROUP * i : GROUP * (i + 1), 2 * S * fy : 2 * S * (fy + 1)
                ]
    out_ref[...] = rows_ref[...].astype(bf16).reshape(GROUP, GROUP, 2 * S)


def shift_matrix(d):
    k = np.arange(S) - S // 2
    x = np.arange(S)
    return np.exp(2j * np.pi * k * x[:, None] / S) @ np.exp(-2j * np.pi * k[:, None] * (x + d) / S) / S


def plane_group():
    return [
        ((x + PLANE_X) % 4) * N_WA + (wa + PLANE_WA) % N_WA for x in range(4) for wa in range(N_WA)
    ]


def line_group():
    return [(z + LINE_Z) % FACETS for z in range(FACETS)]


def left_shifts():
    order = np.array([2 * dest + i for i in range(2) for dest in plane_group()])
    tables = []
    for fx in range(4):
        shift = shift_matrix((fx + 0.5) / 4)[order] * SCALE
        table = np.concatenate([shift.real, shift.imag], axis=1).astype(np.float32)
        high = table.astype(jnp.bfloat16)
        low = (table - high.astype(np.float32)).astype(jnp.bfloat16)
        tables.append(np.concatenate([high, low], axis=0))
    return np.stack(tables)


def right_shifts():
    tables = []
    for fy in range(4):
        shift = shift_matrix((fy + 0.5) / 4).T
        tables.append(
            np.concatenate(
                [
                    np.concatenate([shift.real, shift.imag], axis=1),
                    np.concatenate([-shift.imag, shift.real], axis=1),
                ],
                axis=0,
            )
        )
    table = np.stack(tables).astype(np.float32)
    high = table.astype(jnp.bfloat16)
    return np.concatenate([high, (table - high.astype(np.float32)).astype(jnp.bfloat16)], axis=2)


def middle_kernel(in_ref, shift_ref, out_ref):
    total = in_ref[0].astype(f32)
    for k in range(1, GROUP):
        total = total + in_ref[k].astype(f32)
    for fy in range(4):
        high, low = split_bf16(total[8 * fy : 8 * (fy + 1)])
        both = jnp.concatenate([high, low], axis=0)
        products = jnp.dot(both, shift_ref[(fy + LINE_Z // 4) % 4], preferred_element_type=f32)
        out_ref[8 * fy : 8 * (fy + 1), :] = (
            products[:8, : 2 * S] + products[:8, 2 * S :] + products[8:, : 2 * S]
        )


VMEM = pl.BlockSpec(memory_space=pltpu.VMEM)
SMEM = pl.BlockSpec(memory_space=pltpu.SMEM)


def shards(
    visibilities,
    visibility_uv_offsets,
    block_owner_index,
    block_cell_number,
    live_counts,
    touch_lists,
):
    range_index = lax.axis_index("wa")
    touch_group = [((z + TOUCH_Z) % 16) * 4 + (x + TOUCH_X) % 4 for z in range(16) for x in range(4)]
    named = lax.all_to_all(
        jnp.broadcast_to(touch_lists[None], (N_COL, DEVICE_COLUMNS, TOUCH)),
        ("z", "x"),
        split_axis=0,
        concat_axis=0,
        axis_index_groups=[touch_group],
        tiled=True,
    ).reshape(N_COL * DEVICE_COLUMNS, TOUCH)
    cells = block_cell_number.reshape(1, DEVICE_SLOTS)
    shape = 4 * DEVICE_SLOTS + 8
    half = 2 * DEVICE_SLOTS
    packed = (
        jnp.pad(visibilities.reshape(half, BLOCK_VISIBILITY), ((0, shape - half), (0, 0))).astype(f32)
        + jnp.pad(
            visibility_uv_offsets.reshape(half, BLOCK_VISIBILITY), ((half, 8), (0, 0))
        ).astype(f32)
        + jnp.pad(
            cells, ((2 * half, 7), (0, BLOCK_VISIBILITY - DEVICE_SLOTS))
        ).astype(f32)
    )
    towers = pl.pallas_call(
        grid_kernel,
        out_shape=jax.ShapeDtypeStruct((S * DEVICE_SLOTS, 2 * S), f32),
        in_specs=[SMEM, VMEM],
        out_specs=VMEM,
        scratch_shapes=[
            pltpu.VMEM((8, BLOCK_VISIBILITY), jnp.int32),
            pltpu.SMEM((8, BLOCK_VISIBILITY), jnp.int32),
            pltpu.VMEM((2 * DEVICE_SLOTS, BLOCK_VISIBILITY), f32),
            pltpu.VMEM((2 * DEVICE_SLOTS, BLOCK_VISIBILITY), f32),
            pltpu.VMEM((RANGE_PLANES, S, 2 * S), f32),
            pltpu.VMEM((RANGE_PLANES, S, 2 * S), f32),
            pltpu.SemaphoreType.DMA,
        ],
        compiler_params=pltpu.CompilerParams(vmem_limit_bytes=48 * 1024 * 1024),
        cost_estimate=pl.CostEstimate(
            flops=300_000_000, bytes_accessed=2_200_000, transcendentals=0
        ),
        name="grid_blocks",
    )(
        (range_index * RANGE_PLANES).reshape(1).astype(jnp.int32),
        packed,
    )
    partial_rows = pl.pallas_call(
        facet_kernel,
        out_shape=jax.ShapeDtypeStruct((GROUP, GROUP, 2 * S), bf16),
        in_specs=[SMEM, VMEM, VMEM, VMEM, VMEM, VMEM],
        out_specs=VMEM,
        scratch_shapes=[
            pltpu.VMEM((FACETS * S, 2 * S), f32),
            pltpu.VMEM((FACETS * S, 2 * S), f32),
        ],
        compiler_params=pltpu.CompilerParams(vmem_limit_bytes=24 * 1024 * 1024),
        name="facet_sums",
    )(
        live_counts.reshape(1),
        block_owner_index.reshape(1, DEVICE_SLOTS),
        cells,
        named,
        jnp.asarray(left_shifts()),
        towers,
    )
    arrived = lax.all_to_all(
        partial_rows,
        ("x", "wa"),
        split_axis=0,
        concat_axis=0,
        axis_index_groups=[plane_group()],
        tiled=True,
    )
    plane_rows = pl.pallas_call(
        middle_kernel,
        out_shape=jax.ShapeDtypeStruct((GROUP, 2 * S), f32),
        in_specs=[VMEM, VMEM],
        out_specs=VMEM,
        name="plane_sums",
    )(arrived, jnp.asarray(right_shifts()))
    arrived = lax.all_to_all(
        plane_rows.reshape(FACETS, 2, 2 * S),
        "z",
        split_axis=0,
        concat_axis=0,
        axis_index_groups=[line_group()],
        tiled=True,
    )
    return jnp.sum(arrived, axis=0)


def solution(mesh):
    grid = Mesh(mesh.devices.reshape(16, 4, N_WA), ("z", "x", "wa"))
    col = ("z", "x")
    placed = (
        P(col, "wa", None, None, None),
        P(col, "wa", None, None, None),
        P(col, "wa", None, None),
        P(col, "wa", None),
        P(col, "wa"),
        P(col, None),
    )
    return jax.shard_map(
        shards, mesh=grid, in_specs=placed, out_specs=P(("z", "x", "wa"), None), check_vma=False
    )
```

```python
import functools
import math

import jax
import jax.numpy as jnp
import numpy as np
from jax import lax
from jax.experimental import pallas as pl
from jax.experimental.pallas import tpu as pltpu
from jax.sharding import Mesh, PartitionSpec as P

S = 64
BLOCK_VISIBILITY = 128
RANGE_PLANES = 16
FACETS = 16
TOUCH = 12
DEVICE_COLUMNS = 2
COLUMN_SUBGRIDS = 32
DEVICE_SLOTS = 64
N_COL = 64
N_WA = 8

FULL_TURN = 2.0 * math.pi
FIELD_WIDTH = 0.2
CELL_STEP = 0.37
WTERM_LIMIT = 4000.0
SCALE = 1.0 / math.sqrt(BLOCK_VISIBILITY * N_COL * N_WA * DEVICE_SLOTS)
CELLS = DEVICE_COLUMNS * COLUMN_SUBGRIDS * RANGE_PLANES
UNROLL = 8
GROUP = 32
TOUCH_Z, TOUCH_X = 10, 2
PLANE_X, PLANE_WA = 2, 4
LINE_Z = 8

f32 = jnp.float32
bf16 = jnp.bfloat16


def half_turn_fits():
    nodes = np.cos(np.pi * (np.arange(400) + 0.5) / 400) * 0.125 + 0.125
    root = np.sqrt(nodes)
    sine = np.polynomial.chebyshev.Chebyshev.fit(nodes, np.sin(np.pi * root) / root, 4, domain=[0, 0.25])
    cosine = np.polynomial.chebyshev.Chebyshev.fit(nodes, np.cos(np.pi * root), 5, domain=[0, 0.25])
    return tuple(
        [float(c) for c in fit.convert(kind=np.polynomial.Polynomial).coef] for fit in (sine, cosine)
    )


SINE_FIT, COSINE_FIT = half_turn_fits()


def horner(fit, z):
    total = fit[-1]
    for c in fit[-2::-1]:
        total = total * z + c
    return total


def cos_sin_turns(turns):
    h = turns - jnp.floor(turns + 0.5)
    z = h * h
    sine = h * horner(SINE_FIT, z)
    cosine = horner(COSINE_FIT, z)
    return 1.0 - 2.0 * (sine * sine), 2.0 * (sine * cosine)


def plane_place(k):
    return ((k // N_WA + PLANE_X) % 4) * N_WA + (k + PLANE_WA) % N_WA


def plane_group():
    return [plane_place(k) for k in range(GROUP)]


def line_group():
    return [(z + LINE_Z) % FACETS for z in range(FACETS)]


def shift_parts(difference, d):
    h = (difference.astype(f32) - d) * (1.0 / S)
    h = h - jnp.floor(h + 0.5)
    z = h * h
    cotangent = horner(COSINE_FIT, z) / (h * horner(SINE_FIT, z))
    scale = jnp.where(difference & 1 == 0, -math.sin(math.pi * d) / S, math.sin(math.pi * d) / S)
    return scale * cotangent, -scale


def make_shifts(left_ref, right_ref):
    r = lax.broadcasted_iota(jnp.int32, (S, 2 * S), 0)
    lane = lax.broadcasted_iota(jnp.int32, (S, 2 * S), 1)
    x = 2 * plane_place(r & (GROUP - 1)) + r // GROUP
    for fx in range(4):
        real, imag = shift_parts(x - (lane & (S - 1)), (fx + 0.5) / 4)
        high, low = split_bf16(jnp.where(lane < S, real, imag) * SCALE)
        left_ref[fx] = jnp.concatenate([high, low], axis=0)
    m = lax.broadcasted_iota(jnp.int32, (2 * S, 2 * S), 0)
    lane = lax.broadcasted_iota(jnp.int32, (2 * S, 2 * S), 1)
    for fy in range(4):
        real, imag = shift_parts((lane & (S - 1)) - (m & (S - 1)), (fy + 0.5) / 4)
        imag = jnp.where(m < S, imag, -imag)
        high, low = split_bf16(jnp.where((m < S) == (lane < S), real, imag))
        right_ref[fy] = jnp.concatenate([high, low], axis=1)


def grid_kernel(
    packed_ref,
    out_ref,
    phase_ref,
    chosen_ref,
    left_ref,
    right_ref,
    cell_row,
    cells,
    vis_rows,
    uv_rows,
    screen_a,
    screen_b,
    arrival,
):
    labels = packed_ref[4 * DEVICE_SLOTS : 4 * DEVICE_SLOTS + 8, :].astype(jnp.int32)
    cell_row[...] = labels
    copy = pltpu.make_async_copy(cell_row, cells, arrival)
    copy.start()
    label = labels[0:1, :DEVICE_SLOTS]
    owner = labels[1:2, :DEVICE_SLOTS]
    column_half = (label // (COLUMN_SUBGRIDS * RANGE_PLANES)) % DEVICE_COLUMNS
    row = (label // RANGE_PLANES) % COLUMN_SUBGRIDS
    column = owner * DEVICE_COLUMNS + column_half
    columns = DEVICE_COLUMNS * N_COL

    facet = lax.broadcasted_iota(jnp.int32, (FACETS, 1), 0)
    fx = (facet % 4).astype(f32)
    fy = (facet // 4).astype(f32)
    turns = CELL_STEP * (
        (column.astype(f32) - columns / 2 + 0.5) * ((fx - 1.5) / 4)
        + (row.astype(f32) - COLUMN_SUBGRIDS / 2 + 0.5) * ((fy - 1.5) / 4)
    )
    cosine, sine = cos_sin_turns(turns)
    phase_ref[:FACETS] = cosine
    phase_ref[FACETS:] = sine

    place = ((owner // 4 + 16 - TOUCH_Z) % 16) * 4 + (owner + 4 - TOUCH_X) % 4
    place = place * DEVICE_COLUMNS + column_half
    chosen = lax.broadcasted_iota(jnp.int32, (columns, DEVICE_SLOTS), 0) == place
    alive = lax.broadcasted_iota(jnp.int32, (1, DEVICE_SLOTS), 1) < labels[2:3, :DEVICE_SLOTS]
    chosen_ref[...] = jnp.where(chosen & alive, 1.0, 0.0).astype(bf16)

    make_shifts(left_ref, right_ref)
    vis_rows[...] = packed_ref[: 2 * DEVICE_SLOTS, :]
    uv_rows[...] = packed_ref[2 * DEVICE_SLOTS : 4 * DEVICE_SLOTS, :]

    lane = lax.broadcasted_iota(jnp.int32, (S, 2 * S), 1)
    a = (lax.broadcasted_iota(jnp.int32, (S, 2 * S), 0) - S // 2).astype(f32) * (FIELD_WIDTH / S)
    e = ((lane & (S - 1)) - S // 2).astype(f32) * (FIELD_WIDTH / S)
    radius = a * a + e * e
    lag = -radius / (1.0 + jnp.sqrt(1.0 - radius))
    sign = jnp.where(lane < S, -1.0, 1.0).astype(f32)
    plane_step = 2.0 * WTERM_LIMIT / (RANGE_PLANES * N_WA)
    first_plane = labels[0:1, :] // CELLS * RANGE_PLANES

    def make_screen(p, carry):
        depth = -WTERM_LIMIT + ((first_plane + p).astype(f32) + 0.5) * plane_step
        cosine, sine = cos_sin_turns(depth * lag)
        screen_a[p] = cosine
        screen_b[p] = sine * sign
        return carry

    lax.fori_loop(0, RANGE_PLANES, make_screen, 0)

    copy.wait()

    fine = lax.broadcasted_iota(jnp.int32, (8, 1), 0).astype(f32) * (1.0 / S)
    coarse = (lax.broadcasted_iota(jnp.int32, (8, 1), 0) - 4).astype(f32) * (8.0 / S)

    def one_block(b):
        u = uv_rows[pl.ds(2 * b, 1), :]
        v = uv_rows[pl.ds(2 * b + 1, 1), :]
        vr = vis_rows[pl.ds(2 * b, 1), :]
        vi = vis_rows[pl.ds(2 * b + 1, 1), :]
        turns = jnp.concatenate([u * fine, u * coarse, v * fine, v * coarse], axis=0)
        c, s = cos_sin_turns(turns)
        cu, su, cua, sua = c[0:8], s[0:8], c[8:16], s[8:16]
        cv, sv, cva, sva = c[16:24], s[16:24], c[24:32], s[24:32]
        wra = vr * cva - vi * sva
        wia = vr * sva + vi * cva
        uc, us, wr, wi = [], [], [], []
        for k in range(8):
            ck, sk = cua[k : k + 1], sua[k : k + 1]
            uc.append(ck * cu - sk * su)
            us.append(sk * cu + ck * su)
            rk, ik = wra[k : k + 1], wia[k : k + 1]
            wr.append(rk * cv - ik * sv)
            wi.append(rk * sv + ik * cv)
        uc, us, wr, wi = [jnp.concatenate(t, axis=0).astype(bf16) for t in (uc, us, wr, wi)]
        left = jnp.concatenate([uc, us], axis=1)
        right = jnp.concatenate(
            [jnp.concatenate([wr, -wi], axis=1), jnp.concatenate([wi, wr], axis=1)], axis=0
        )
        grid = lax.dot_general(
            left, right, (((1,), (1,)), ((), ())), preferred_element_type=f32
        )
        plane = cells[0, b] & (RANGE_PLANES - 1)
        towers = grid * screen_a[plane] + pltpu.roll(grid, S, 1) * screen_b[plane]
        out_ref[pl.ds(b, S, stride=DEVICE_SLOTS), :] = towers

    def some_blocks(i, carry):
        for k in range(UNROLL):
            one_block(i * UNROLL + k)
        return carry

    lax.fori_loop(0, DEVICE_SLOTS // UNROLL, some_blocks, 0)


def split_bf16(x):
    high = x.astype(bf16)
    return high, (x - high.astype(f32)).astype(bf16)


def facet_kernel(
    phase_ref, chosen_ref, touch_ref, left_ref, right_ref, towers_ref, out_ref, facet_ref, rows_ref
):
    columns = DEVICE_COLUMNS * N_COL
    named = touch_ref[...].astype(f32)
    facet_lane = lax.broadcasted_iota(jnp.int32, (columns, FACETS), 1).astype(f32)
    touched = named[:, 0:1] == facet_lane
    for t in range(1, TOUCH):
        touched = touched | (named[:, t : t + 1] == facet_lane)
    touched = jnp.where(touched, 1.0, 0.0).astype(bf16)
    mask = lax.dot_general(
        touched, chosen_ref[...], (((0,), (0,)), ((), ())), preferred_element_type=f32
    )
    weights = phase_ref[...] * jnp.concatenate([mask, mask], axis=0)
    high, low = split_bf16(weights)
    left = jnp.concatenate(
        [jnp.concatenate([high, high], axis=1), jnp.concatenate([low, jnp.zeros_like(low)], axis=1)],
        axis=0,
    )
    sign = jnp.where(lax.broadcasted_iota(jnp.int32, (FACETS, 2 * S), 1) < S, -1.0, 1.0).astype(f32)

    for l in range(0, S, 2):
        pair = jnp.concatenate(
            [
                towers_ref[l * DEVICE_SLOTS : (l + 1) * DEVICE_SLOTS, :],
                towers_ref[(l + 1) * DEVICE_SLOTS : (l + 2) * DEVICE_SLOTS, :],
            ],
            axis=1,
        )
        high, low = split_bf16(pair)
        sums = jnp.dot(left, jnp.concatenate([high, low], axis=0), preferred_element_type=f32)
        sums = sums[: 2 * FACETS] + sums[2 * FACETS :]
        for k in range(2):
            part = sums[:, 2 * S * k : 2 * S * (k + 1)]
            facet_ref[pl.ds(l + k, FACETS, stride=S), :] = (
                part[:FACETS] + sign * pltpu.roll(part[FACETS:], S, 1)
            )

    wide = jnp.where(lax.broadcasted_iota(jnp.int32, (S, 2 * S), 1) < S, -1.0, 1.0).astype(f32)
    for fx in range(4):
        plain = [facet_ref[(fx + 4 * fy) * S : (fx + 4 * fy + 1) * S, :] for fy in range(4)]
        turned = [wide * pltpu.roll(g, S, 1) for g in plain]
        stack = jnp.concatenate(
            [jnp.concatenate(plain, axis=1), jnp.concatenate(turned, axis=1)], axis=0
        )
        high, low = split_bf16(stack)
        shift = left_ref[fx]
        first = jnp.dot(shift, high, preferred_element_type=f32)
        second = jnp.dot(shift[:S], low, preferred_element_type=f32)
        half = first[:S] + first[S:] + second
        for fy in range(4):
            high, low = split_bf16(half[:, 2 * S * fy : 2 * S * (fy + 1)])
            products = jnp.dot(
                jnp.concatenate([high, low], axis=0), right_ref[fy], preferred_element_type=f32
            )
            image = products[:S, : 2 * S] + products[:S, 2 * S :] + products[S:, : 2 * S]
            place = (fx + 4 * fy - LINE_Z) % FACETS
            for i in range(2):
                rows_ref[pl.ds(2 * place + i, GROUP, stride=GROUP), :] = image[
                    GROUP * i : GROUP * (i + 1)
                ]
    out_ref[...] = rows_ref[...].astype(bf16).reshape(GROUP, GROUP, 2 * S)


VMEM = pl.BlockSpec(memory_space=pltpu.VMEM)


def shards(
    visibilities,
    visibility_uv_offsets,
    block_owner_index,
    block_cell_number,
    live_counts,
    touch_lists,
):
    range_index = lax.axis_index("wa")
    touch_group = [((z + TOUCH_Z) % 16) * 4 + (x + TOUCH_X) % 4 for z in range(16) for x in range(4)]
    named = lax.all_to_all(
        jnp.broadcast_to(touch_lists[None].astype(bf16), (N_COL, DEVICE_COLUMNS, TOUCH)),
        ("z", "x"),
        split_axis=0,
        concat_axis=0,
        axis_index_groups=[touch_group],
        tiled=True,
    ).reshape(N_COL * DEVICE_COLUMNS, TOUCH)
    cells = block_cell_number.reshape(1, DEVICE_SLOTS)
    shape = 4 * DEVICE_SLOTS + 8
    half = 2 * DEVICE_SLOTS
    lanes = (0, BLOCK_VISIBILITY - DEVICE_SLOTS)
    row = lax.broadcasted_iota(jnp.int32, (shape, BLOCK_VISIBILITY), 0)
    packed = (
        jnp.pad(visibilities.reshape(half, BLOCK_VISIBILITY), ((0, shape - half), (0, 0))).astype(f32)
        + jnp.pad(
            visibility_uv_offsets.reshape(half, BLOCK_VISIBILITY), ((half, 8), (0, 0))
        ).astype(f32)
        + jnp.pad(cells, ((2 * half, 7), lanes)).astype(f32)
        + jnp.pad(block_owner_index.reshape(1, DEVICE_SLOTS), ((2 * half + 1, 6), lanes)).astype(f32)
        + jnp.where(row == 2 * half, (CELLS * range_index).astype(f32), 0.0)
        + jnp.where(row == 2 * half + 2, live_counts[0, 0].astype(f32), 0.0)
    )
    towers, phases, chosen, left, right = pl.pallas_call(
        grid_kernel,
        out_shape=(
            jax.ShapeDtypeStruct((S * DEVICE_SLOTS, 2 * S), f32),
            jax.ShapeDtypeStruct((2 * FACETS, DEVICE_SLOTS), f32),
            jax.ShapeDtypeStruct((DEVICE_COLUMNS * N_COL, DEVICE_SLOTS), bf16),
            jax.ShapeDtypeStruct((4, 2 * S, 2 * S), bf16),
            jax.ShapeDtypeStruct((4, 2 * S, 4 * S), bf16),
        ),
        in_specs=[VMEM],
        out_specs=(VMEM,) * 5,
        scratch_shapes=[
            pltpu.VMEM((8, BLOCK_VISIBILITY), jnp.int32),
            pltpu.SMEM((8, BLOCK_VISIBILITY), jnp.int32),
            pltpu.VMEM((2 * DEVICE_SLOTS, BLOCK_VISIBILITY), f32),
            pltpu.VMEM((2 * DEVICE_SLOTS, BLOCK_VISIBILITY), f32),
            pltpu.VMEM((RANGE_PLANES, S, 2 * S), f32),
            pltpu.VMEM((RANGE_PLANES, S, 2 * S), f32),
            pltpu.SemaphoreType.DMA,
        ],
        compiler_params=pltpu.CompilerParams(vmem_limit_bytes=48 * 1024 * 1024),
        cost_estimate=pl.CostEstimate(
            flops=300_000_000, bytes_accessed=2_200_000, transcendentals=0
        ),
        name="grid_blocks",
    )(
        packed,
    )
    partial_rows = pl.pallas_call(
        facet_kernel,
        out_shape=jax.ShapeDtypeStruct((GROUP, GROUP, 2 * S), bf16),
        in_specs=[VMEM] * 6,
        out_specs=VMEM,
        scratch_shapes=[
            pltpu.VMEM((FACETS * S, 2 * S), f32),
            pltpu.VMEM((FACETS * S, 2 * S), f32),
        ],
        compiler_params=pltpu.CompilerParams(vmem_limit_bytes=24 * 1024 * 1024),
        name="facet_sums",
    )(
        phases,
        chosen,
        named,
        left,
        right,
        towers,
    )
    arrived = lax.all_to_all(
        partial_rows,
        ("x", "wa"),
        split_axis=0,
        concat_axis=0,
        axis_index_groups=[plane_group()],
        tiled=True,
    )
    plane_rows = jnp.sum(arrived.astype(f32), axis=0)
    arrived = lax.all_to_all(
        plane_rows.reshape(FACETS, 2, 2 * S),
        "z",
        split_axis=0,
        concat_axis=0,
        axis_index_groups=[line_group()],
        tiled=True,
    )
    return jnp.sum(arrived, axis=0)


def solution(mesh):
    grid = Mesh(mesh.devices.reshape(16, 4, N_WA), ("z", "x", "wa"))
    col = ("z", "x")
    placed = (
        P(col, "wa", None, None, None),
        P(col, "wa", None, None, None),
        P(col, "wa", None, None),
        P(col, "wa", None),
        P(col, "wa"),
        P(col, None),
    )
    return jax.shard_map(
        shards, mesh=grid, in_specs=placed, out_specs=P(("z", "x", "wa"), None), check_vma=False
    )
```

```python
import functools
import math

import jax
import jax.numpy as jnp
import numpy as np
from jax import lax
from jax.experimental import pallas as pl
from jax.experimental.pallas import tpu as pltpu
from jax.sharding import Mesh, PartitionSpec as P

S = 64
BLOCK_VISIBILITY = 128
RANGE_PLANES = 16
FACETS = 16
TOUCH = 12
DEVICE_COLUMNS = 2
COLUMN_SUBGRIDS = 32
DEVICE_SLOTS = 64
N_COL = 64
N_WA = 8

FULL_TURN = 2.0 * math.pi
FIELD_WIDTH = 0.2
CELL_STEP = 0.37
WTERM_LIMIT = 4000.0
SCALE = 1.0 / math.sqrt(BLOCK_VISIBILITY * N_COL * N_WA * DEVICE_SLOTS)
UNROLL = 8
GROUP = 32
TOUCH_Z, TOUCH_X = 11, 2
PLANE_X, PLANE_WA = 2, 4
LINE_Z = 8

f32 = jnp.float32
bf16 = jnp.bfloat16


def half_turn_fits():
    nodes = np.cos(np.pi * (np.arange(400) + 0.5) / 400) * 0.125 + 0.125
    root = np.sqrt(nodes)
    sine = np.polynomial.chebyshev.Chebyshev.fit(nodes, np.sin(np.pi * root) / root, 4, domain=[0, 0.25])
    cosine = np.polynomial.chebyshev.Chebyshev.fit(nodes, np.cos(np.pi * root), 4, domain=[0, 0.25])
    return tuple(
        [float(c) for c in fit.convert(kind=np.polynomial.Polynomial).coef] for fit in (sine, cosine)
    )


SINE_FIT, COSINE_FIT = half_turn_fits()


def horner(fit, z):
    total = fit[-1]
    for c in fit[-2::-1]:
        total = total * z + c
    return total


def cos_sin_turns(turns):
    h = turns - jnp.floor(turns + 0.5)
    z = h * h
    sine = h * horner(SINE_FIT, z)
    cosine = horner(COSINE_FIT, z)
    return 1.0 - 2.0 * (sine * sine), 2.0 * (sine * cosine)


def plane_place(k):
    return ((k // N_WA + PLANE_X) % 4) * N_WA + (k + PLANE_WA) % N_WA


def plane_group():
    return [plane_place(k) for k in range(GROUP)]


def line_group():
    return [(z + LINE_Z) % FACETS for z in range(FACETS)]


def shift_parts(difference, d):
    h = (difference.astype(f32) - d) * (1.0 / S)
    h = h - jnp.floor(h + 0.5)
    z = h * h
    cotangent = horner(COSINE_FIT, z) / (h * horner(SINE_FIT, z))
    scale = jnp.where(difference & 1 == 0, -math.sin(math.pi * d) / S, math.sin(math.pi * d) / S)
    return scale * cotangent, -scale


def make_shifts(left_ref, right_ref):
    r = lax.broadcasted_iota(jnp.int32, (S, 2 * S), 0)
    lane = lax.broadcasted_iota(jnp.int32, (S, 2 * S), 1)
    x = 2 * plane_place(r & (GROUP - 1)) + r // GROUP
    for fx in range(4):
        real, imag = shift_parts(x - (lane & (S - 1)), (fx + 0.5) / 4)
        high, low = split_bf16(jnp.where(lane < S, real, imag) * SCALE)
        left_ref[fx] = jnp.concatenate([high, low], axis=0)
    m = lax.broadcasted_iota(jnp.int32, (2 * S, 2 * S), 0)
    lane = lax.broadcasted_iota(jnp.int32, (2 * S, 2 * S), 1)
    for fy in range(4):
        real, imag = shift_parts((lane & (S - 1)) - (m & (S - 1)), (fy + 0.5) / 4)
        imag = jnp.where(m < S, imag, -imag)
        high, low = split_bf16(jnp.where((m < S) == (lane < S), real, imag))
        right_ref[fy] = jnp.concatenate([high, low], axis=1)


def grid_kernel(
    packed_ref,
    out_ref,
    phase_ref,
    chosen_ref,
    left_ref,
    right_ref,
    cell_row,
    cells,
    vis_rows,
    uv_rows,
    screen_a,
    screen_b,
    arrival,
):
    labels = packed_ref[4 * DEVICE_SLOTS : 4 * DEVICE_SLOTS + 8, :].astype(jnp.int32)
    cell_row[...] = labels
    copy = pltpu.make_async_copy(cell_row, cells, arrival)
    copy.start()
    label = labels[0:1, :DEVICE_SLOTS]
    owner = labels[1:2, :DEVICE_SLOTS]
    column_half = (label // (COLUMN_SUBGRIDS * RANGE_PLANES)) % DEVICE_COLUMNS
    row = (label // RANGE_PLANES) % COLUMN_SUBGRIDS
    column = owner * DEVICE_COLUMNS + column_half
    columns = DEVICE_COLUMNS * N_COL

    facet = lax.broadcasted_iota(jnp.int32, (FACETS, 1), 0)
    fx = (facet % 4).astype(f32)
    fy = (facet // 4).astype(f32)
    turns = CELL_STEP * (
        (column.astype(f32) - columns / 2 + 0.5) * ((fx - 1.5) / 4)
        + (row.astype(f32) - COLUMN_SUBGRIDS / 2 + 0.5) * ((fy - 1.5) / 4)
    )
    cosine, sine = cos_sin_turns(turns)
    phase_ref[:FACETS] = cosine
    phase_ref[FACETS:] = sine

    place = ((owner // 4 + 16 - TOUCH_Z) % 16) * 4 + (owner + 4 - TOUCH_X) % 4
    place = place * DEVICE_COLUMNS + column_half
    chosen = lax.broadcasted_iota(jnp.int32, (columns, DEVICE_SLOTS), 0) == place
    alive = lax.broadcasted_iota(jnp.int32, (1, DEVICE_SLOTS), 1) < labels[2:3, 0:1]
    chosen_ref[...] = jnp.where(chosen & alive, 1.0, 0.0).astype(bf16)

    make_shifts(left_ref, right_ref)
    vis_rows[...] = packed_ref[: 2 * DEVICE_SLOTS, :]
    uv_rows[...] = packed_ref[2 * DEVICE_SLOTS : 4 * DEVICE_SLOTS, :]

    lane = lax.broadcasted_iota(jnp.int32, (S, 2 * S), 1)
    a = (lax.broadcasted_iota(jnp.int32, (S, 2 * S), 0) - S // 2).astype(f32) * (FIELD_WIDTH / S)
    e = ((lane & (S - 1)) - S // 2).astype(f32) * (FIELD_WIDTH / S)
    radius = a * a + e * e
    lag = -radius / (1.0 + jnp.sqrt(1.0 - radius))
    sign = jnp.where(lane < S, -1.0, 1.0).astype(f32)
    plane_step = 2.0 * WTERM_LIMIT / (RANGE_PLANES * N_WA)
    first_plane = (labels[3:4, 0:1] * RANGE_PLANES).astype(f32)
    first_turns = (-WTERM_LIMIT + (first_plane + 0.5) * plane_step) * lag
    step_turns = plane_step * lag

    def make_screen(p, carry):
        cosine, sine = cos_sin_turns(first_turns + p.astype(f32) * step_turns)
        screen_a[p] = cosine
        screen_b[p] = sine * sign
        return carry

    lax.fori_loop(0, RANGE_PLANES, make_screen, 0)

    copy.wait()

    fine = lax.broadcasted_iota(jnp.int32, (8, 1), 0).astype(f32) * (1.0 / S)
    coarse = (lax.broadcasted_iota(jnp.int32, (8, 1), 0) - 4).astype(f32) * (8.0 / S)

    def one_block(b):
        u = uv_rows[pl.ds(2 * b, 1), :]
        v = uv_rows[pl.ds(2 * b + 1, 1), :]
        vr = vis_rows[pl.ds(2 * b, 1), :]
        vi = vis_rows[pl.ds(2 * b + 1, 1), :]
        turns = jnp.concatenate([u * fine, u * coarse, v * fine, v * coarse], axis=0)
        c, s = cos_sin_turns(turns)
        cu, su, cua, sua = c[0:8], s[0:8], c[8:16], s[8:16]
        cv, sv, cva, sva = c[16:24], s[16:24], c[24:32], s[24:32]
        wra = vr * cva - vi * sva
        wia = vr * sva + vi * cva
        uc, us, wr, wi = [], [], [], []
        for k in range(8):
            ck, sk = cua[k : k + 1], sua[k : k + 1]
            uc.append(ck * cu - sk * su)
            us.append(sk * cu + ck * su)
            rk, ik = wra[k : k + 1], wia[k : k + 1]
            wr.append(rk * cv - ik * sv)
            wi.append(rk * sv + ik * cv)
        uc, us, wr, wi = [jnp.concatenate(t, axis=0).astype(bf16) for t in (uc, us, wr, wi)]
        left = jnp.concatenate([uc, us], axis=1)
        right = jnp.concatenate(
            [jnp.concatenate([wr, -wi], axis=1), jnp.concatenate([wi, wr], axis=1)], axis=0
        )
        grid = lax.dot_general(
            left, right, (((1,), (1,)), ((), ())), preferred_element_type=f32
        )
        plane = cells[0, b] & (RANGE_PLANES - 1)
        towers = grid * screen_a[plane] + pltpu.roll(grid, S, 1) * screen_b[plane]
        out_ref[pl.ds(b, S, stride=DEVICE_SLOTS), :] = towers

    def some_blocks(i, carry):
        for k in range(UNROLL):
            one_block(i * UNROLL + k)
        return carry

    lax.fori_loop(0, DEVICE_SLOTS // UNROLL, some_blocks, 0)


def split_bf16(x):
    high = x.astype(bf16)
    return high, (x - high.astype(f32)).astype(bf16)


def facet_kernel(
    phase_ref, chosen_ref, touch_ref, left_ref, right_ref, towers_ref, out_ref, facet_ref, rows_ref
):
    columns = DEVICE_COLUMNS * N_COL
    named = touch_ref[...].astype(f32)
    facet_lane = lax.broadcasted_iota(jnp.int32, (columns, FACETS), 1).astype(f32)
    touched = named[:, 0:1] == facet_lane
    for t in range(1, TOUCH):
        touched = touched | (named[:, t : t + 1] == facet_lane)
    touched = jnp.where(touched, 1.0, 0.0).astype(bf16)
    mask = lax.dot_general(
        touched, chosen_ref[...], (((0,), (0,)), ((), ())), preferred_element_type=f32
    )
    weights = phase_ref[...] * jnp.concatenate([mask, mask], axis=0)
    high, low = split_bf16(weights)
    left = jnp.concatenate(
        [jnp.concatenate([high, high], axis=1), jnp.concatenate([low, jnp.zeros_like(low)], axis=1)],
        axis=0,
    )
    sign = jnp.where(lax.broadcasted_iota(jnp.int32, (FACETS, 2 * S), 1) < S, -1.0, 1.0).astype(f32)

    for l in range(0, S, 2):
        pair = jnp.concatenate(
            [
                towers_ref[l * DEVICE_SLOTS : (l + 1) * DEVICE_SLOTS, :],
                towers_ref[(l + 1) * DEVICE_SLOTS : (l + 2) * DEVICE_SLOTS, :],
            ],
            axis=1,
        )
        high, low = split_bf16(pair)
        sums = jnp.dot(left, jnp.concatenate([high, low], axis=0), preferred_element_type=f32)
        sums = sums[: 2 * FACETS] + sums[2 * FACETS :]
        for k in range(2):
            part = sums[:, 2 * S * k : 2 * S * (k + 1)]
            facet_ref[pl.ds(l + k, FACETS, stride=S), :] = (
                part[:FACETS] + sign * pltpu.roll(part[FACETS:], S, 1)
            )

    shifted = []
    for fy in range(4):
        high, low = split_bf16(facet_ref[4 * S * fy : 4 * S * (fy + 1), :])
        first = jnp.dot(high, right_ref[fy], preferred_element_type=f32)
        second = jnp.dot(low, right_ref[fy, :, : 2 * S], preferred_element_type=f32)
        shifted.append(first[:, : 2 * S] + first[:, 2 * S :] + second)

    wide = jnp.where(lax.broadcasted_iota(jnp.int32, (S, 2 * S), 1) < S, -1.0, 1.0).astype(f32)
    for fx in range(4):
        plain = [rows[S * fx : S * (fx + 1)] for rows in shifted]
        turned = [wide * pltpu.roll(g, S, 1) for g in plain]
        stack = jnp.concatenate(
            [jnp.concatenate(plain, axis=1), jnp.concatenate(turned, axis=1)], axis=0
        )
        high, low = split_bf16(stack)
        shift = left_ref[fx]
        first = jnp.dot(shift, high, preferred_element_type=f32)
        second = jnp.dot(shift[:S], low, preferred_element_type=f32)
        image = first[:S] + first[S:] + second
        for fy in range(4):
            place = (fx + 4 * fy - LINE_Z) % FACETS
            for i in range(2):
                rows_ref[pl.ds(2 * place + i, GROUP, stride=GROUP), :] = image[
                    GROUP * i : GROUP * (i + 1), 2 * S * fy : 2 * S * (fy + 1)
                ]
    out_ref[...] = rows_ref[...].astype(bf16).reshape(GROUP, GROUP, 2 * S)


VMEM = pl.BlockSpec(memory_space=pltpu.VMEM)


def shards(
    visibilities,
    visibility_uv_offsets,
    block_owner_index,
    block_cell_number,
    live_counts,
    touch_lists,
):
    range_index = lax.axis_index("wa")
    touch_group = [((z + TOUCH_Z) % 16) * 4 + (x + TOUCH_X) % 4 for z in range(16) for x in range(4)]
    named = lax.all_to_all(
        jnp.broadcast_to(touch_lists[None].astype(bf16), (N_COL, DEVICE_COLUMNS, TOUCH)),
        ("z", "x"),
        split_axis=0,
        concat_axis=0,
        axis_index_groups=[touch_group],
        tiled=True,
    ).reshape(N_COL * DEVICE_COLUMNS, TOUCH)
    cells = block_cell_number.reshape(1, DEVICE_SLOTS)
    shape = 4 * DEVICE_SLOTS + 8
    half = 2 * DEVICE_SLOTS
    lanes = (0, BLOCK_VISIBILITY - DEVICE_SLOTS)
    packed = (
        jnp.pad(visibilities.reshape(half, BLOCK_VISIBILITY), ((0, shape - half), (0, 0))).astype(f32)
        + jnp.pad(
            visibility_uv_offsets.reshape(half, BLOCK_VISIBILITY), ((half, 8), (0, 0))
        ).astype(f32)
        + jnp.pad(cells, ((2 * half, 7), lanes)).astype(f32)
        + jnp.pad(block_owner_index.reshape(1, DEVICE_SLOTS), ((2 * half + 1, 6), lanes)).astype(f32)
        + jnp.pad(live_counts, ((2 * half + 2, 5), (0, BLOCK_VISIBILITY - 1))).astype(f32)
        + jnp.pad(
            range_index.reshape(1, 1).astype(jnp.int32),
            ((2 * half + 3, 4), (0, BLOCK_VISIBILITY - 1)),
        ).astype(f32)
    )
    towers, phases, chosen, left, right = pl.pallas_call(
        grid_kernel,
        out_shape=(
            jax.ShapeDtypeStruct((S * DEVICE_SLOTS, 2 * S), f32),
            jax.ShapeDtypeStruct((2 * FACETS, DEVICE_SLOTS), f32),
            jax.ShapeDtypeStruct((DEVICE_COLUMNS * N_COL, DEVICE_SLOTS), bf16),
            jax.ShapeDtypeStruct((4, 2 * S, 2 * S), bf16),
            jax.ShapeDtypeStruct((4, 2 * S, 4 * S), bf16),
        ),
        in_specs=[VMEM],
        out_specs=(VMEM,) * 5,
        scratch_shapes=[
            pltpu.VMEM((8, BLOCK_VISIBILITY), jnp.int32),
            pltpu.SMEM((8, BLOCK_VISIBILITY), jnp.int32),
            pltpu.VMEM((2 * DEVICE_SLOTS, BLOCK_VISIBILITY), f32),
            pltpu.VMEM((2 * DEVICE_SLOTS, BLOCK_VISIBILITY), f32),
            pltpu.VMEM((RANGE_PLANES, S, 2 * S), f32),
            pltpu.VMEM((RANGE_PLANES, S, 2 * S), f32),
            pltpu.SemaphoreType.DMA,
        ],
        compiler_params=pltpu.CompilerParams(vmem_limit_bytes=48 * 1024 * 1024),
        cost_estimate=pl.CostEstimate(
            flops=300_000_000, bytes_accessed=2_200_000, transcendentals=0
        ),
        name="grid_blocks",
    )(
        packed,
    )
    partial_rows = pl.pallas_call(
        facet_kernel,
        out_shape=jax.ShapeDtypeStruct((GROUP, GROUP, 2 * S), bf16),
        in_specs=[VMEM] * 6,
        out_specs=VMEM,
        scratch_shapes=[
            pltpu.VMEM((FACETS * S, 2 * S), f32),
            pltpu.VMEM((FACETS * S, 2 * S), f32),
        ],
        compiler_params=pltpu.CompilerParams(vmem_limit_bytes=24 * 1024 * 1024),
        name="facet_sums",
    )(
        phases,
        chosen,
        named,
        left,
        right,
        towers,
    )
    arrived = lax.all_to_all(
        partial_rows,
        ("x", "wa"),
        split_axis=0,
        concat_axis=0,
        axis_index_groups=[plane_group()],
        tiled=True,
    )
    plane_rows = jnp.sum(arrived.astype(f32), axis=0)
    arrived = lax.all_to_all(
        plane_rows.reshape(FACETS, 2, 2 * S),
        "z",
        split_axis=0,
        concat_axis=0,
        axis_index_groups=[line_group()],
        tiled=True,
    )
    return jnp.sum(arrived, axis=0)


def solution(mesh):
    grid = Mesh(mesh.devices.reshape(16, 4, N_WA), ("z", "x", "wa"))
    col = ("z", "x")
    placed = (
        P(col, "wa", None, None, None),
        P(col, "wa", None, None, None),
        P(col, "wa", None, None),
        P(col, "wa", None),
        P(col, "wa"),
        P(col, None),
    )
    return jax.shard_map(
        shards, mesh=grid, in_specs=placed, out_specs=P(("z", "x", "wa"), None), check_vma=False
    )
```

```python
import functools
import math

import jax
import jax.numpy as jnp
import numpy as np
from jax import lax
from jax.experimental import pallas as pl
from jax.experimental.pallas import tpu as pltpu
from jax.sharding import Mesh, PartitionSpec as P

S = 64
BLOCK_VISIBILITY = 128
RANGE_PLANES = 16
FACETS = 16
TOUCH = 12
DEVICE_COLUMNS = 2
COLUMN_SUBGRIDS = 32
DEVICE_SLOTS = 64
N_COL = 64
N_WA = 8

FULL_TURN = 2.0 * math.pi
FIELD_WIDTH = 0.2
CELL_STEP = 0.37
WTERM_LIMIT = 4000.0
SCALE = 1.0 / math.sqrt(BLOCK_VISIBILITY * N_COL * N_WA * DEVICE_SLOTS)
UNROLL = 8
GROUP = 32
TOUCH_Z, TOUCH_X = 11, 2
PLANE_X, PLANE_WA = 2, 4
LINE_Z = 8

f32 = jnp.float32
bf16 = jnp.bfloat16


def half_turn_fits():
    nodes = np.cos(np.pi * (np.arange(400) + 0.5) / 400) * 0.125 + 0.125
    root = np.sqrt(nodes)
    sine = np.polynomial.chebyshev.Chebyshev.fit(nodes, np.sin(np.pi * root) / root, 4, domain=[0, 0.25])
    cosine = np.polynomial.chebyshev.Chebyshev.fit(nodes, np.cos(np.pi * root), 4, domain=[0, 0.25])
    return tuple(
        [float(c) for c in fit.convert(kind=np.polynomial.Polynomial).coef] for fit in (sine, cosine)
    )


SINE_FIT, COSINE_FIT = half_turn_fits()


def horner(fit, z):
    total = fit[-1]
    for c in fit[-2::-1]:
        total = total * z + c
    return total


def cos_sin_turns(turns):
    h = turns - jnp.floor(turns + 0.5)
    z = h * h
    sine = h * horner(SINE_FIT, z)
    cosine = horner(COSINE_FIT, z)
    return 1.0 - 2.0 * (sine * sine), 2.0 * (sine * cosine)


def plane_place(k):
    return ((k // N_WA + PLANE_X) % 4) * N_WA + (k + PLANE_WA) % N_WA


def plane_group():
    return [plane_place(k) for k in range(GROUP)]


def line_group():
    return [(z + LINE_Z) % FACETS for z in range(FACETS)]


def shift_parts(difference, d):
    h = (difference.astype(f32) - d) * (1.0 / S)
    h = h - jnp.floor(h + 0.5)
    z = h * h
    cotangent = horner(COSINE_FIT, z) / (h * horner(SINE_FIT, z))
    scale = jnp.where(difference & 1 == 0, -math.sin(math.pi * d) / S, math.sin(math.pi * d) / S)
    return scale * cotangent, -scale


def make_shifts(left_ref, right_ref):
    r = lax.broadcasted_iota(jnp.int32, (S, 2 * S), 0)
    lane = lax.broadcasted_iota(jnp.int32, (S, 2 * S), 1)
    x = 2 * plane_place(r & (GROUP - 1)) + r // GROUP
    for fx in range(4):
        real, imag = shift_parts(x - (lane & (S - 1)), (fx + 0.5) / 4)
        high, low = split_bf16(jnp.where(lane < S, real, imag) * SCALE)
        left_ref[fx] = jnp.concatenate([high, low], axis=0)
    m = lax.broadcasted_iota(jnp.int32, (2 * S, 2 * S), 0)
    lane = lax.broadcasted_iota(jnp.int32, (2 * S, 2 * S), 1)
    for fy in range(4):
        real, imag = shift_parts((lane & (S - 1)) - (m & (S - 1)), (fy + 0.5) / 4)
        imag = jnp.where(m < S, imag, -imag)
        high, low = split_bf16(jnp.where((m < S) == (lane < S), real, imag))
        right_ref[fy] = jnp.concatenate([high, low], axis=1)


def grid_kernel(
    packed_ref,
    out_ref,
    phase_ref,
    chosen_ref,
    left_ref,
    right_ref,
    cell_row,
    cells,
    screen_a,
    screen_b,
    arrival,
):
    labels = packed_ref[4 * DEVICE_SLOTS : 4 * DEVICE_SLOTS + 8, :].astype(jnp.int32)
    cell_row[...] = labels
    copy = pltpu.make_async_copy(cell_row, cells, arrival)
    copy.start()
    label = labels[0:1, :DEVICE_SLOTS]
    owner = labels[1:2, :DEVICE_SLOTS]
    column_half = (label // (COLUMN_SUBGRIDS * RANGE_PLANES)) % DEVICE_COLUMNS
    row = (label // RANGE_PLANES) % COLUMN_SUBGRIDS
    column = owner * DEVICE_COLUMNS + column_half
    columns = DEVICE_COLUMNS * N_COL

    facet = lax.broadcasted_iota(jnp.int32, (FACETS, 1), 0)
    fx = (facet % 4).astype(f32)
    fy = (facet // 4).astype(f32)
    turns = CELL_STEP * (
        (column.astype(f32) - columns / 2 + 0.5) * ((fx - 1.5) / 4)
        + (row.astype(f32) - COLUMN_SUBGRIDS / 2 + 0.5) * ((fy - 1.5) / 4)
    )
    cosine, sine = cos_sin_turns(turns)
    phase_ref[:FACETS] = cosine
    phase_ref[FACETS:] = sine

    place = ((owner // 4 + 16 - TOUCH_Z) % 16) * 4 + (owner + 4 - TOUCH_X) % 4
    place = place * DEVICE_COLUMNS + column_half
    chosen = lax.broadcasted_iota(jnp.int32, (columns, DEVICE_SLOTS), 0) == place
    alive = lax.broadcasted_iota(jnp.int32, (1, DEVICE_SLOTS), 1) < labels[2:3, 0:1]
    chosen_ref[...] = jnp.where(chosen & alive, 1.0, 0.0).astype(bf16)

    make_shifts(left_ref, right_ref)

    lane = lax.broadcasted_iota(jnp.int32, (S, 2 * S), 1)
    a = (lax.broadcasted_iota(jnp.int32, (S, 2 * S), 0) - S // 2).astype(f32) * (FIELD_WIDTH / S)
    e = ((lane & (S - 1)) - S // 2).astype(f32) * (FIELD_WIDTH / S)
    radius = a * a + e * e
    lag = -radius / (1.0 + jnp.sqrt(1.0 - radius))
    sign = jnp.where(lane < S, -1.0, 1.0).astype(f32)
    plane_step = 2.0 * WTERM_LIMIT / (RANGE_PLANES * N_WA)
    first_plane = (labels[3:4, 0:1] * RANGE_PLANES).astype(f32)
    first_turns = (-WTERM_LIMIT + (first_plane + 0.5) * plane_step) * lag
    step_turns = plane_step * lag

    def make_screen(p, carry):
        cosine, sine = cos_sin_turns(first_turns + p.astype(f32) * step_turns)
        screen_a[p] = cosine
        screen_b[p] = sine * sign
        return carry

    lax.fori_loop(0, RANGE_PLANES, make_screen, 0)

    copy.wait()

    fine = lax.broadcasted_iota(jnp.int32, (8, 1), 0).astype(f32) * (1.0 / S)
    coarse = (lax.broadcasted_iota(jnp.int32, (8, 1), 0) - 4).astype(f32) * (8.0 / S)

    def one_block(b):
        u = packed_ref[pl.ds(2 * DEVICE_SLOTS + 2 * b, 1), :]
        v = packed_ref[pl.ds(2 * DEVICE_SLOTS + 2 * b + 1, 1), :]
        vr = packed_ref[pl.ds(2 * b, 1), :]
        vi = packed_ref[pl.ds(2 * b + 1, 1), :]
        turns = jnp.concatenate([u * fine, u * coarse, v * fine, v * coarse], axis=0)
        c, s = cos_sin_turns(turns)
        cu, su, cua, sua = c[0:8], s[0:8], c[8:16], s[8:16]
        cv, sv, cva, sva = c[16:24], s[16:24], c[24:32], s[24:32]
        wra = vr * cva - vi * sva
        wia = vr * sva + vi * cva
        uc, us, wr, wi = [], [], [], []
        for k in range(8):
            ck, sk = cua[k : k + 1], sua[k : k + 1]
            uc.append(ck * cu - sk * su)
            us.append(sk * cu + ck * su)
            rk, ik = wra[k : k + 1], wia[k : k + 1]
            wr.append(rk * cv - ik * sv)
            wi.append(rk * sv + ik * cv)
        uc, us, wr, wi = [jnp.concatenate(t, axis=0).astype(bf16) for t in (uc, us, wr, wi)]
        left = jnp.concatenate([uc, us], axis=1)
        right = jnp.concatenate(
            [jnp.concatenate([wr, -wi], axis=1), jnp.concatenate([wi, wr], axis=1)], axis=0
        )
        grid = lax.dot_general(
            left, right, (((1,), (1,)), ((), ())), preferred_element_type=f32
        )
        plane = cells[0, b] & (RANGE_PLANES - 1)
        towers = grid * screen_a[plane] + pltpu.roll(grid, S, 1) * screen_b[plane]
        out_ref[pl.ds(b, S, stride=DEVICE_SLOTS), :] = towers

    def some_blocks(i, carry):
        for k in range(UNROLL):
            one_block(i * UNROLL + k)
        return carry

    lax.fori_loop(0, DEVICE_SLOTS // UNROLL, some_blocks, 0)


def split_bf16(x):
    high = x.astype(bf16)
    return high, (x - high.astype(f32)).astype(bf16)


def facet_kernel(
    phase_ref, chosen_ref, touch_ref, left_ref, right_ref, towers_ref, out_ref, facet_ref, rows_ref
):
    columns = DEVICE_COLUMNS * N_COL
    named = touch_ref[...].astype(f32).T
    facet = lax.broadcasted_iota(jnp.int32, (FACETS, columns), 0).astype(f32)
    touched = named[0:1] == facet
    for t in range(1, TOUCH):
        touched = touched | (named[t : t + 1] == facet)
    touched = jnp.where(touched, 1.0, 0.0).astype(bf16)
    mask = jnp.dot(touched, chosen_ref[...], preferred_element_type=f32)
    weights = phase_ref[...] * jnp.concatenate([mask, mask], axis=0)
    high, low = split_bf16(weights)
    left = jnp.concatenate(
        [jnp.concatenate([high, high], axis=1), jnp.concatenate([low, jnp.zeros_like(low)], axis=1)],
        axis=0,
    )
    sign = jnp.where(lax.broadcasted_iota(jnp.int32, (FACETS, 2 * S), 1) < S, -1.0, 1.0).astype(f32)

    for l in range(0, S, 2):
        pair = jnp.concatenate(
            [
                towers_ref[l * DEVICE_SLOTS : (l + 1) * DEVICE_SLOTS, :],
                towers_ref[(l + 1) * DEVICE_SLOTS : (l + 2) * DEVICE_SLOTS, :],
            ],
            axis=1,
        )
        high, low = split_bf16(pair)
        sums = jnp.dot(left, jnp.concatenate([high, low], axis=0), preferred_element_type=f32)
        sums = sums[: 2 * FACETS] + sums[2 * FACETS :]
        for k in range(2):
            part = sums[:, 2 * S * k : 2 * S * (k + 1)]
            facet_ref[pl.ds(l + k, FACETS, stride=S), :] = (
                part[:FACETS] + sign * pltpu.roll(part[FACETS:], S, 1)
            )

    shifted = []
    for fy in range(4):
        high, low = split_bf16(facet_ref[4 * S * fy : 4 * S * (fy + 1), :])
        first = jnp.dot(high, right_ref[fy], preferred_element_type=f32)
        second = jnp.dot(low, right_ref[fy, :, : 2 * S], preferred_element_type=f32)
        shifted.append(first[:, : 2 * S] + first[:, 2 * S :] + second)

    wide = jnp.where(lax.broadcasted_iota(jnp.int32, (S, 2 * S), 1) < S, -1.0, 1.0).astype(f32)
    for fx in range(4):
        plain = [rows[S * fx : S * (fx + 1)] for rows in shifted]
        turned = [wide * pltpu.roll(g, S, 1) for g in plain]
        stack = jnp.concatenate(
            [jnp.concatenate(plain, axis=1), jnp.concatenate(turned, axis=1)], axis=0
        )
        high, low = split_bf16(stack)
        shift = left_ref[fx]
        first = jnp.dot(shift, high, preferred_element_type=f32)
        second = jnp.dot(shift[:S], low, preferred_element_type=f32)
        image = first[:S] + first[S:] + second
        for fy in range(4):
            place = (fx + 4 * fy - LINE_Z) % FACETS
            for i in range(2):
                rows_ref[pl.ds(2 * place + i, GROUP, stride=GROUP), :] = image[
                    GROUP * i : GROUP * (i + 1), 2 * S * fy : 2 * S * (fy + 1)
                ]
    out_ref[...] = rows_ref[: FACETS * S].astype(bf16).reshape(GROUP, GROUP, 2 * S)


VMEM = pl.BlockSpec(memory_space=pltpu.VMEM)


def shards(
    visibilities,
    visibility_uv_offsets,
    block_owner_index,
    block_cell_number,
    live_counts,
    touch_lists,
):
    range_index = lax.axis_index("wa")
    touch_group = [((z + TOUCH_Z) % 16) * 4 + (x + TOUCH_X) % 4 for z in range(16) for x in range(4)]
    named = lax.all_to_all(
        jnp.broadcast_to(touch_lists[None].astype(bf16), (N_COL, DEVICE_COLUMNS, TOUCH)),
        ("z", "x"),
        split_axis=0,
        concat_axis=0,
        axis_index_groups=[touch_group],
        tiled=True,
    ).reshape(N_COL * DEVICE_COLUMNS, TOUCH)
    cells = block_cell_number.reshape(1, DEVICE_SLOTS)
    shape = 4 * DEVICE_SLOTS + 8
    half = 2 * DEVICE_SLOTS
    lanes = (0, BLOCK_VISIBILITY - DEVICE_SLOTS)
    packed = (
        jnp.pad(visibilities.reshape(half, BLOCK_VISIBILITY), ((0, shape - half), (0, 0))).astype(f32)
        + jnp.pad(
            visibility_uv_offsets.reshape(half, BLOCK_VISIBILITY), ((half, 8), (0, 0))
        ).astype(f32)
        + jnp.pad(cells, ((2 * half, 7), lanes)).astype(f32)
        + jnp.pad(block_owner_index.reshape(1, DEVICE_SLOTS), ((2 * half + 1, 6), lanes)).astype(f32)
        + jnp.pad(live_counts, ((2 * half + 2, 5), (0, BLOCK_VISIBILITY - 1))).astype(f32)
        + jnp.pad(
            range_index.reshape(1, 1).astype(jnp.int32),
            ((2 * half + 3, 4), (0, BLOCK_VISIBILITY - 1)),
        ).astype(f32)
    )
    towers, phases, chosen, left, right = pl.pallas_call(
        grid_kernel,
        out_shape=(
            jax.ShapeDtypeStruct(((S + 1) * DEVICE_SLOTS, 2 * S), f32),
            jax.ShapeDtypeStruct((2 * FACETS, DEVICE_SLOTS), f32),
            jax.ShapeDtypeStruct((DEVICE_COLUMNS * N_COL, DEVICE_SLOTS), bf16),
            jax.ShapeDtypeStruct((4, 2 * S, 2 * S), bf16),
            jax.ShapeDtypeStruct((4, 2 * S, 4 * S), bf16),
        ),
        in_specs=[VMEM],
        out_specs=(VMEM,) * 5,
        scratch_shapes=[
            pltpu.VMEM((8, BLOCK_VISIBILITY), jnp.int32),
            pltpu.SMEM((8, BLOCK_VISIBILITY), jnp.int32),
            pltpu.VMEM((RANGE_PLANES, S, 2 * S), f32),
            pltpu.VMEM((RANGE_PLANES, S, 2 * S), f32),
            pltpu.SemaphoreType.DMA,
        ],
        compiler_params=pltpu.CompilerParams(vmem_limit_bytes=48 * 1024 * 1024),
        cost_estimate=pl.CostEstimate(
            flops=300_000_000, bytes_accessed=2_200_000, transcendentals=0
        ),
        name="grid_blocks",
    )(
        packed,
    )
    partial_rows = pl.pallas_call(
        facet_kernel,
        out_shape=jax.ShapeDtypeStruct((GROUP, GROUP, 2 * S), bf16),
        in_specs=[VMEM] * 6,
        out_specs=VMEM,
        scratch_shapes=[
            pltpu.VMEM((FACETS * S + S, 2 * S), f32),
            pltpu.VMEM((FACETS * S + GROUP, 2 * S), f32),
        ],
        compiler_params=pltpu.CompilerParams(vmem_limit_bytes=24 * 1024 * 1024),
        name="facet_sums",
    )(
        phases,
        chosen,
        named,
        left,
        right,
        towers,
    )
    arrived = lax.all_to_all(
        partial_rows,
        ("x", "wa"),
        split_axis=0,
        concat_axis=0,
        axis_index_groups=[plane_group()],
        tiled=True,
    )
    plane_rows = jnp.sum(arrived.astype(f32), axis=0)
    arrived = lax.all_to_all(
        plane_rows.reshape(FACETS, 2, 2 * S),
        "z",
        split_axis=0,
        concat_axis=0,
        axis_index_groups=[line_group()],
        tiled=True,
    )
    return jnp.sum(arrived, axis=0)


def solution(mesh):
    grid = Mesh(mesh.devices.reshape(16, 4, N_WA), ("z", "x", "wa"))
    col = ("z", "x")
    placed = (
        P(col, "wa", None, None, None),
        P(col, "wa", None, None, None),
        P(col, "wa", None, None),
        P(col, "wa", None),
        P(col, "wa"),
        P(col, None),
    )
    return jax.shard_map(
        shards, mesh=grid, in_specs=placed, out_specs=P(("z", "x", "wa"), None), check_vma=False
    )
```

```python
import functools
import math

import jax
import jax.numpy as jnp
import numpy as np
from jax import lax
from jax.experimental import pallas as pl
from jax.experimental.pallas import tpu as pltpu
from jax.sharding import Mesh, PartitionSpec as P

S = 64
BLOCK_VISIBILITY = 128
RANGE_PLANES = 16
FACETS = 16
TOUCH = 12
DEVICE_COLUMNS = 2
COLUMN_SUBGRIDS = 32
DEVICE_SLOTS = 64
N_COL = 64
N_WA = 8

FULL_TURN = 2.0 * math.pi
FIELD_WIDTH = 0.2
CELL_STEP = 0.37
WTERM_LIMIT = 4000.0
SCALE = 1.0 / math.sqrt(BLOCK_VISIBILITY * N_COL * N_WA * DEVICE_SLOTS)
UNROLL = 16
GROUP = 32
TOUCH_Z, TOUCH_X = 11, 2
PLANE_X, PLANE_WA = 2, 4
LINE_Z = 8

f32 = jnp.float32
bf16 = jnp.bfloat16


def half_turn_fits():
    nodes = np.cos(np.pi * (np.arange(400) + 0.5) / 400) * 0.125 + 0.125
    root = np.sqrt(nodes)
    sine = np.polynomial.chebyshev.Chebyshev.fit(nodes, np.sin(np.pi * root) / root, 4, domain=[0, 0.25])
    cosine = np.polynomial.chebyshev.Chebyshev.fit(nodes, np.cos(np.pi * root), 4, domain=[0, 0.25])
    return tuple(
        [float(c) for c in fit.convert(kind=np.polynomial.Polynomial).coef] for fit in (sine, cosine)
    )


SINE_FIT, COSINE_FIT = half_turn_fits()


def horner(fit, z):
    total = fit[-1]
    for c in fit[-2::-1]:
        total = total * z + c
    return total


def cos_sin_turns(turns):
    h = turns - jnp.floor(turns + 0.5)
    z = h * h
    sine = h * horner(SINE_FIT, z)
    cosine = horner(COSINE_FIT, z)
    return 1.0 - 2.0 * (sine * sine), 2.0 * (sine * cosine)


def plane_place(k):
    return ((k // N_WA + PLANE_X) % 4) * N_WA + (k + PLANE_WA) % N_WA


def plane_group():
    return [plane_place(k) for k in range(GROUP)]


def line_group():
    return [(z + LINE_Z) % FACETS for z in range(FACETS)]


def shift_parts(difference, d):
    h = (difference.astype(f32) - d) * (1.0 / S)
    h = h - jnp.floor(h + 0.5)
    z = h * h
    cotangent = horner(COSINE_FIT, z) / (h * horner(SINE_FIT, z))
    scale = jnp.where(difference & 1 == 0, -math.sin(math.pi * d) / S, math.sin(math.pi * d) / S)
    return scale * cotangent, -scale


def make_shifts(left_ref, right_ref):
    r = lax.broadcasted_iota(jnp.int32, (S, 2 * S), 0)
    lane = lax.broadcasted_iota(jnp.int32, (S, 2 * S), 1)
    x = 2 * plane_place(r & (GROUP - 1)) + r // GROUP
    for fx in range(4):
        real, imag = shift_parts(x - (lane & (S - 1)), (fx + 0.5) / 4)
        high, low = split_bf16(jnp.where(lane < S, real, imag) * SCALE)
        left_ref[fx] = jnp.concatenate([high, low], axis=0)
    m = lax.broadcasted_iota(jnp.int32, (2 * S, 2 * S), 0)
    lane = lax.broadcasted_iota(jnp.int32, (2 * S, 2 * S), 1)
    for fy in range(4):
        real, imag = shift_parts((lane & (S - 1)) - (m & (S - 1)), (fy + 0.5) / 4)
        imag = jnp.where(m < S, imag, -imag)
        high, low = split_bf16(jnp.where((m < S) == (lane < S), real, imag))
        right_ref[fy] = jnp.concatenate([high, low], axis=1)


def grid_kernel(
    packed_ref,
    out_ref,
    phase_ref,
    chosen_ref,
    left_ref,
    right_ref,
    cell_row,
    cells,
    screen_a,
    screen_b,
    arrival,
):
    labels = packed_ref[4 * DEVICE_SLOTS : 4 * DEVICE_SLOTS + 8, :].astype(jnp.int32)
    cell_row[...] = labels
    copy = pltpu.make_async_copy(cell_row, cells, arrival)
    copy.start()
    label = labels[0:1, :DEVICE_SLOTS]
    owner = labels[1:2, :DEVICE_SLOTS]
    column_half = (label // (COLUMN_SUBGRIDS * RANGE_PLANES)) % DEVICE_COLUMNS
    row = (label // RANGE_PLANES) % COLUMN_SUBGRIDS
    column = owner * DEVICE_COLUMNS + column_half
    columns = DEVICE_COLUMNS * N_COL

    facet = lax.broadcasted_iota(jnp.int32, (FACETS, 1), 0)
    fx = (facet % 4).astype(f32)
    fy = (facet // 4).astype(f32)
    turns = CELL_STEP * (
        (column.astype(f32) - columns / 2 + 0.5) * ((fx - 1.5) / 4)
        + (row.astype(f32) - COLUMN_SUBGRIDS / 2 + 0.5) * ((fy - 1.5) / 4)
    )
    cosine, sine = cos_sin_turns(turns)
    phase_ref[:FACETS] = cosine
    phase_ref[FACETS:] = sine

    place = ((owner // 4 + 16 - TOUCH_Z) % 16) * 4 + (owner + 4 - TOUCH_X) % 4
    place = place * DEVICE_COLUMNS + column_half
    chosen = lax.broadcasted_iota(jnp.int32, (columns, DEVICE_SLOTS), 0) == place
    chosen_ref[...] = jnp.where(chosen, 1.0, 0.0).astype(bf16)

    make_shifts(left_ref, right_ref)

    lane = lax.broadcasted_iota(jnp.int32, (S, 2 * S), 1)
    a = (lax.broadcasted_iota(jnp.int32, (S, 2 * S), 0) - S // 2).astype(f32) * (FIELD_WIDTH / S)
    e = ((lane & (S - 1)) - S // 2).astype(f32) * (FIELD_WIDTH / S)
    radius = a * a + e * e
    lag = -radius / (1.0 + jnp.sqrt(1.0 - radius))
    sign = jnp.where(lane < S, -1.0, 1.0).astype(f32)
    plane_step = 2.0 * WTERM_LIMIT / (RANGE_PLANES * N_WA)
    first_plane = (labels[2:3, 0:1] * RANGE_PLANES).astype(f32)
    first_turns = (-WTERM_LIMIT + (first_plane + 0.5) * plane_step) * lag
    step_turns = plane_step * lag

    def make_screen(p, carry):
        cosine, sine = cos_sin_turns(first_turns + p.astype(f32) * step_turns)
        screen_a[p] = cosine
        screen_b[p] = sine * sign
        return carry

    lax.fori_loop(0, RANGE_PLANES, make_screen, 0)

    copy.wait()

    fine = lax.broadcasted_iota(jnp.int32, (8, 1), 0).astype(f32) * (1.0 / S)
    coarse = (lax.broadcasted_iota(jnp.int32, (8, 1), 0) - 4).astype(f32) * (8.0 / S)

    def one_block(b):
        u = packed_ref[pl.ds(2 * DEVICE_SLOTS + 2 * b, 1), :]
        v = packed_ref[pl.ds(2 * DEVICE_SLOTS + 2 * b + 1, 1), :]
        vr = packed_ref[pl.ds(2 * b, 1), :]
        vi = packed_ref[pl.ds(2 * b + 1, 1), :]
        turns = jnp.concatenate([u * fine, u * coarse, v * fine, v * coarse], axis=0)
        c, s = cos_sin_turns(turns)
        cu, su, cua, sua = c[0:8], s[0:8], c[8:16], s[8:16]
        cv, sv, cva, sva = c[16:24], s[16:24], c[24:32], s[24:32]
        wra = vr * cva - vi * sva
        wia = vr * sva + vi * cva
        uc, us, wr, wi = [], [], [], []
        for k in range(8):
            ck, sk = cua[k : k + 1], sua[k : k + 1]
            uc.append(ck * cu - sk * su)
            us.append(sk * cu + ck * su)
            rk, ik = wra[k : k + 1], wia[k : k + 1]
            wr.append(rk * cv - ik * sv)
            wi.append(rk * sv + ik * cv)
        uc, us, wr, wi = [jnp.concatenate(t, axis=0).astype(bf16) for t in (uc, us, wr, wi)]
        left = jnp.concatenate([uc, us], axis=1)
        right = jnp.concatenate(
            [jnp.concatenate([wr, -wi], axis=1), jnp.concatenate([wi, wr], axis=1)], axis=0
        )
        grid = lax.dot_general(
            left, right, (((1,), (1,)), ((), ())), preferred_element_type=f32
        )
        plane = cells[0, b] & (RANGE_PLANES - 1)
        towers = grid * screen_a[plane] + pltpu.roll(grid, S, 1) * screen_b[plane]
        out_ref[pl.ds(b, S, stride=DEVICE_SLOTS), :] = towers

    def some_blocks(i, carry):
        for k in range(UNROLL):
            one_block(i * UNROLL + k)
        return carry

    lax.fori_loop(0, DEVICE_SLOTS // UNROLL, some_blocks, 0)


def split_bf16(x):
    high = x.astype(bf16)
    return high, (x - high.astype(f32)).astype(bf16)


def facet_kernel(
    live_ref, phase_ref, chosen_ref, touch_ref, left_ref, right_ref, towers_ref, out_ref, facet_ref, rows_ref
):
    columns = DEVICE_COLUMNS * N_COL
    named = touch_ref[...].astype(f32).T
    facet = lax.broadcasted_iota(jnp.int32, (FACETS, columns), 0).astype(f32)
    touched = named[0:1] == facet
    for t in range(1, TOUCH):
        touched = touched | (named[t : t + 1] == facet)
    touched = jnp.where(touched, 1.0, 0.0).astype(bf16)
    mask = jnp.dot(touched, chosen_ref[...], preferred_element_type=f32)
    slot = lax.broadcasted_iota(jnp.int32, (FACETS, DEVICE_SLOTS), 1)
    mask = jnp.where(slot < live_ref[...], mask, 0.0)
    weights = phase_ref[...] * jnp.concatenate([mask, mask], axis=0)
    high, low = split_bf16(weights)
    left = jnp.concatenate(
        [jnp.concatenate([high, high], axis=1), jnp.concatenate([low, jnp.zeros_like(low)], axis=1)],
        axis=0,
    )
    sign = jnp.where(lax.broadcasted_iota(jnp.int32, (FACETS, 2 * S), 1) < S, -1.0, 1.0).astype(f32)

    for l in range(0, S, 2):
        pair = jnp.concatenate(
            [
                towers_ref[l * DEVICE_SLOTS : (l + 1) * DEVICE_SLOTS, :],
                towers_ref[(l + 1) * DEVICE_SLOTS : (l + 2) * DEVICE_SLOTS, :],
            ],
            axis=1,
        )
        high, low = split_bf16(pair)
        sums = jnp.dot(left, jnp.concatenate([high, low], axis=0), preferred_element_type=f32)
        sums = sums[: 2 * FACETS] + sums[2 * FACETS :]
        for k in range(2):
            part = sums[:, 2 * S * k : 2 * S * (k + 1)]
            facet_ref[pl.ds(l + k, FACETS, stride=S), :] = (
                part[:FACETS] + sign * pltpu.roll(part[FACETS:], S, 1)
            )

    shifted = []
    for fy in range(4):
        high, low = split_bf16(facet_ref[4 * S * fy : 4 * S * (fy + 1), :])
        first = jnp.dot(high, right_ref[fy], preferred_element_type=f32)
        second = jnp.dot(low, right_ref[fy, :, : 2 * S], preferred_element_type=f32)
        shifted.append(first[:, : 2 * S] + first[:, 2 * S :] + second)

    wide = jnp.where(lax.broadcasted_iota(jnp.int32, (S, 2 * S), 1) < S, -1.0, 1.0).astype(f32)
    for fx in range(4):
        plain = [rows[S * fx : S * (fx + 1)] for rows in shifted]
        turned = [wide * pltpu.roll(g, S, 1) for g in plain]
        stack = jnp.concatenate(
            [jnp.concatenate(plain, axis=1), jnp.concatenate(turned, axis=1)], axis=0
        )
        high, low = split_bf16(stack)
        shift = left_ref[fx]
        first = jnp.dot(shift, high, preferred_element_type=f32)
        second = jnp.dot(shift[:S], low, preferred_element_type=f32)
        image = first[:S] + first[S:] + second
        for fy in range(4):
            place = (fx + 4 * fy - LINE_Z) % FACETS
            for i in range(2):
                rows_ref[pl.ds(2 * place + i, GROUP, stride=GROUP), :] = image[
                    GROUP * i : GROUP * (i + 1), 2 * S * fy : 2 * S * (fy + 1)
                ]
    out_ref[...] = rows_ref[: FACETS * S].astype(bf16).reshape(GROUP, GROUP, 2 * S)


VMEM = pl.BlockSpec(memory_space=pltpu.VMEM)


def shards(
    visibilities,
    visibility_uv_offsets,
    block_owner_index,
    block_cell_number,
    live_counts,
    touch_lists,
):
    range_index = lax.axis_index("wa")
    touch_group = [((z + TOUCH_Z) % 16) * 4 + (x + TOUCH_X) % 4 for z in range(16) for x in range(4)]
    named = lax.all_to_all(
        jnp.broadcast_to(touch_lists[None].astype(bf16), (N_COL, DEVICE_COLUMNS, TOUCH)),
        ("z", "x"),
        split_axis=0,
        concat_axis=0,
        axis_index_groups=[touch_group],
        tiled=True,
    ).reshape(N_COL * DEVICE_COLUMNS, TOUCH)
    cells = block_cell_number.reshape(1, DEVICE_SLOTS)
    shape = 4 * DEVICE_SLOTS + 8
    half = 2 * DEVICE_SLOTS
    lanes = (0, BLOCK_VISIBILITY - DEVICE_SLOTS)
    packed = (
        jnp.pad(visibilities.reshape(half, BLOCK_VISIBILITY), ((0, shape - half), (0, 0))).astype(f32)
        + jnp.pad(
            visibility_uv_offsets.reshape(half, BLOCK_VISIBILITY), ((half, 8), (0, 0))
        ).astype(f32)
        + jnp.pad(cells, ((2 * half, 7), lanes)).astype(f32)
        + jnp.pad(block_owner_index.reshape(1, DEVICE_SLOTS), ((2 * half + 1, 6), lanes)).astype(f32)
        + jnp.pad(
            range_index.reshape(1, 1).astype(jnp.int32),
            ((2 * half + 2, 5), (0, BLOCK_VISIBILITY - 1)),
        ).astype(f32)
    )
    towers, phases, chosen, left, right = pl.pallas_call(
        grid_kernel,
        out_shape=(
            jax.ShapeDtypeStruct(((S + 1) * DEVICE_SLOTS, 2 * S), f32),
            jax.ShapeDtypeStruct((2 * FACETS, DEVICE_SLOTS), f32),
            jax.ShapeDtypeStruct((DEVICE_COLUMNS * N_COL, DEVICE_SLOTS), bf16),
            jax.ShapeDtypeStruct((4, 2 * S, 2 * S), bf16),
            jax.ShapeDtypeStruct((4, 2 * S, 4 * S), bf16),
        ),
        in_specs=[VMEM],
        out_specs=(VMEM,) * 5,
        scratch_shapes=[
            pltpu.VMEM((8, BLOCK_VISIBILITY), jnp.int32),
            pltpu.SMEM((8, BLOCK_VISIBILITY), jnp.int32),
            pltpu.VMEM((RANGE_PLANES, S, 2 * S), f32),
            pltpu.VMEM((RANGE_PLANES, S, 2 * S), f32),
            pltpu.SemaphoreType.DMA,
        ],
        compiler_params=pltpu.CompilerParams(vmem_limit_bytes=48 * 1024 * 1024),
        cost_estimate=pl.CostEstimate(
            flops=300_000_000, bytes_accessed=2_200_000, transcendentals=0
        ),
        name="grid_blocks",
    )(
        packed,
    )
    partial_rows = pl.pallas_call(
        facet_kernel,
        out_shape=jax.ShapeDtypeStruct((GROUP, GROUP, 2 * S), bf16),
        in_specs=[VMEM] * 7,
        out_specs=VMEM,
        scratch_shapes=[
            pltpu.VMEM((FACETS * S + S, 2 * S), f32),
            pltpu.VMEM((FACETS * S + GROUP, 2 * S), f32),
        ],
        compiler_params=pltpu.CompilerParams(vmem_limit_bytes=24 * 1024 * 1024),
        name="facet_sums",
    )(
        live_counts,
        phases,
        chosen,
        named,
        left,
        right,
        towers,
    )
    arrived = lax.all_to_all(
        partial_rows,
        ("x", "wa"),
        split_axis=0,
        concat_axis=0,
        axis_index_groups=[plane_group()],
        tiled=True,
    )
    plane_rows = jnp.sum(arrived.astype(f32), axis=0)
    arrived = lax.all_to_all(
        plane_rows.reshape(FACETS, 2, 2 * S),
        "z",
        split_axis=0,
        concat_axis=0,
        axis_index_groups=[line_group()],
        tiled=True,
    )
    return jnp.sum(arrived, axis=0)


def solution(mesh):
    grid = Mesh(mesh.devices.reshape(16, 4, N_WA), ("z", "x", "wa"))
    col = ("z", "x")
    placed = (
        P(col, "wa", None, None, None),
        P(col, "wa", None, None, None),
        P(col, "wa", None, None),
        P(col, "wa", None),
        P(col, "wa"),
        P(col, None),
    )
    return jax.shard_map(
        shards, mesh=grid, in_specs=placed, out_specs=P(("z", "x", "wa"), None), check_vma=False
    )
```

```python
import functools
import math

import jax
import jax.numpy as jnp
import numpy as np
from jax import lax
from jax.experimental import pallas as pl
from jax.experimental.pallas import tpu as pltpu
from jax.sharding import Mesh, PartitionSpec as P

S = 64
BLOCK_VISIBILITY = 128
RANGE_PLANES = 16
FACETS = 16
TOUCH = 12
DEVICE_COLUMNS = 2
COLUMN_SUBGRIDS = 32
DEVICE_SLOTS = 64
N_COL = 64
N_WA = 8

FULL_TURN = 2.0 * math.pi
FIELD_WIDTH = 0.2
CELL_STEP = 0.37
WTERM_LIMIT = 4000.0
SCALE = 1.0 / math.sqrt(BLOCK_VISIBILITY * N_COL * N_WA * DEVICE_SLOTS)
UNROLL = 16
GROUP = 32
TOUCH_Z, TOUCH_X = 11, 0
PLANE_X, PLANE_WA = 2, 4
LINE_Z = 8

f32 = jnp.float32
bf16 = jnp.bfloat16


def half_turn_fits():
    nodes = np.cos(np.pi * (np.arange(400) + 0.5) / 400) * 0.125 + 0.125
    root = np.sqrt(nodes)
    sine = np.polynomial.chebyshev.Chebyshev.fit(nodes, np.sin(np.pi * root) / root, 4, domain=[0, 0.25])
    cosine = np.polynomial.chebyshev.Chebyshev.fit(nodes, np.cos(np.pi * root), 4, domain=[0, 0.25])
    return tuple(
        [float(c) for c in fit.convert(kind=np.polynomial.Polynomial).coef] for fit in (sine, cosine)
    )


SINE_FIT, COSINE_FIT = half_turn_fits()


def horner(fit, z):
    total = fit[-1]
    for c in fit[-2::-1]:
        total = total * z + c
    return total


def cos_sin_turns(turns):
    h = turns - jnp.floor(turns + 0.5)
    z = h * h
    sine = h * horner(SINE_FIT, z)
    cosine = horner(COSINE_FIT, z)
    return 1.0 - 2.0 * (sine * sine), 2.0 * (sine * cosine)


def plane_place(k):
    return ((k // N_WA + PLANE_X) % 4) * N_WA + (k + PLANE_WA) % N_WA


def plane_group():
    return [plane_place(k) for k in range(GROUP)]


def line_group():
    return [(z + LINE_Z) % FACETS for z in range(FACETS)]


def shift_parts(difference, d):
    h = (difference.astype(f32) - d) * (1.0 / S)
    h = h - jnp.floor(h + 0.5)
    z = h * h
    cotangent = horner(COSINE_FIT, z) / (h * horner(SINE_FIT, z))
    scale = jnp.where(difference & 1 == 0, -math.sin(math.pi * d) / S, math.sin(math.pi * d) / S)
    return scale * cotangent, -scale


def make_shifts(left_ref, right_ref):
    r = lax.broadcasted_iota(jnp.int32, (S, 2 * S), 0)
    lane = lax.broadcasted_iota(jnp.int32, (S, 2 * S), 1)
    x = 2 * plane_place(r & (GROUP - 1)) + r // GROUP
    for fx in range(4):
        real, imag = shift_parts(x - (lane & (S - 1)), (fx + 0.5) / 4)
        high, low = split_bf16(jnp.where(lane < S, real, imag) * SCALE)
        left_ref[fx] = jnp.concatenate([high, low], axis=0)
    m = lax.broadcasted_iota(jnp.int32, (2 * S, 2 * S), 0)
    lane = lax.broadcasted_iota(jnp.int32, (2 * S, 2 * S), 1)
    for fy in range(4):
        real, imag = shift_parts((lane & (S - 1)) - (m & (S - 1)), (fy + 0.5) / 4)
        imag = jnp.where(m < S, imag, -imag)
        high, low = split_bf16(jnp.where((m < S) == (lane < S), real, imag))
        right_ref[fy] = jnp.concatenate([high, low], axis=1)


def grid_kernel(
    packed_ref,
    out_ref,
    phase_ref,
    chosen_ref,
    left_ref,
    right_ref,
    cell_row,
    cells,
    screen_a,
    screen_b,
    arrival,
):
    labels = packed_ref[4 * DEVICE_SLOTS : 4 * DEVICE_SLOTS + 8, :].astype(jnp.int32)
    cell_row[...] = labels
    copy = pltpu.make_async_copy(cell_row, cells, arrival)
    copy.start()
    label = labels[0:1, :DEVICE_SLOTS]
    owner = labels[1:2, :DEVICE_SLOTS]
    column_half = (label // (COLUMN_SUBGRIDS * RANGE_PLANES)) % DEVICE_COLUMNS
    row = (label // RANGE_PLANES) % COLUMN_SUBGRIDS
    column = owner * DEVICE_COLUMNS + column_half
    columns = DEVICE_COLUMNS * N_COL

    facet = lax.broadcasted_iota(jnp.int32, (FACETS, 1), 0)
    fx = (facet % 4).astype(f32)
    fy = (facet // 4).astype(f32)
    turns = CELL_STEP * (
        (column.astype(f32) - columns / 2 + 0.5) * ((fx - 1.5) / 4)
        + (row.astype(f32) - COLUMN_SUBGRIDS / 2 + 0.5) * ((fy - 1.5) / 4)
    )
    cosine, sine = cos_sin_turns(turns)
    phase_ref[:FACETS] = cosine
    phase_ref[FACETS:] = sine

    place = ((owner // 4 + 16 - TOUCH_Z) % 16) * 4 + (owner + 4 - TOUCH_X) % 4
    place = place * DEVICE_COLUMNS + column_half
    chosen = lax.broadcasted_iota(jnp.int32, (columns, DEVICE_SLOTS), 0) == place
    chosen_ref[...] = jnp.where(chosen, 1.0, 0.0).astype(bf16)

    make_shifts(left_ref, right_ref)

    lane = lax.broadcasted_iota(jnp.int32, (S, 2 * S), 1)
    a = (lax.broadcasted_iota(jnp.int32, (S, 2 * S), 0) - S // 2).astype(f32) * (FIELD_WIDTH / S)
    e = ((lane & (S - 1)) - S // 2).astype(f32) * (FIELD_WIDTH / S)
    radius = a * a + e * e
    lag = -radius / (1.0 + jnp.sqrt(1.0 - radius))
    sign = jnp.where(lane < S, -1.0, 1.0).astype(f32)
    plane_step = 2.0 * WTERM_LIMIT / (RANGE_PLANES * N_WA)
    first_plane = (labels[2:3, 0:1] * RANGE_PLANES).astype(f32)
    first_turns = (-WTERM_LIMIT + (first_plane + 0.5) * plane_step) * lag
    step_turns = plane_step * lag

    def make_screen(p, carry):
        cosine, sine = cos_sin_turns(first_turns + p.astype(f32) * step_turns)
        screen_a[p] = cosine
        screen_b[p] = sine * sign
        return carry

    lax.fori_loop(0, RANGE_PLANES, make_screen, 0)

    copy.wait()

    fine = lax.broadcasted_iota(jnp.int32, (8, 1), 0).astype(f32) * (1.0 / S)
    coarse = (lax.broadcasted_iota(jnp.int32, (8, 1), 0) - 4).astype(f32) * (8.0 / S)

    def one_block(b):
        u = packed_ref[pl.ds(2 * DEVICE_SLOTS + 2 * b, 1), :]
        v = packed_ref[pl.ds(2 * DEVICE_SLOTS + 2 * b + 1, 1), :]
        vr = packed_ref[pl.ds(2 * b, 1), :]
        vi = packed_ref[pl.ds(2 * b + 1, 1), :]
        turns = jnp.concatenate([u * fine, u * coarse, v * fine, v * coarse], axis=0)
        c, s = cos_sin_turns(turns)
        cu, su, cua, sua = c[0:8], s[0:8], c[8:16], s[8:16]
        cv, sv, cva, sva = c[16:24], s[16:24], c[24:32], s[24:32]
        wra = vr * cva - vi * sva
        wia = vr * sva + vi * cva
        uc, us, wr, wi = [], [], [], []
        for k in range(8):
            ck, sk = cua[k : k + 1], sua[k : k + 1]
            uc.append(ck * cu - sk * su)
            us.append(sk * cu + ck * su)
            rk, ik = wra[k : k + 1], wia[k : k + 1]
            wr.append(rk * cv - ik * sv)
            wi.append(rk * sv + ik * cv)
        uc, us, wr, wi = [jnp.concatenate(t, axis=0).astype(bf16) for t in (uc, us, wr, wi)]
        left = jnp.concatenate([uc, us], axis=1)
        right = jnp.concatenate(
            [jnp.concatenate([wr, -wi], axis=1), jnp.concatenate([wi, wr], axis=1)], axis=0
        )
        grid = lax.dot_general(
            left, right, (((1,), (1,)), ((), ())), preferred_element_type=f32
        )
        plane = cells[0, b] & (RANGE_PLANES - 1)
        towers = grid * screen_a[plane] + pltpu.roll(grid, S, 1) * screen_b[plane]
        out_ref[pl.ds(b, S, stride=DEVICE_SLOTS), :] = towers

    def some_blocks(i, carry):
        for k in range(UNROLL):
            one_block(i * UNROLL + k)
        return carry

    lax.fori_loop(0, DEVICE_SLOTS // UNROLL, some_blocks, 0)


def split_bf16(x):
    high = x.astype(bf16)
    return high, (x - high.astype(f32)).astype(bf16)


def facet_kernel(
    live_ref, phase_ref, chosen_ref, touch_ref, left_ref, right_ref, towers_ref, out_ref, facet_ref, rows_ref
):
    columns = DEVICE_COLUMNS * N_COL
    named = touch_ref[...].astype(f32).T
    facet = lax.broadcasted_iota(jnp.int32, (FACETS, columns), 0).astype(f32)
    touched = named[0:1] == facet
    for t in range(1, TOUCH):
        touched = touched | (named[t : t + 1] == facet)
    touched = jnp.where(touched, 1.0, 0.0).astype(bf16)
    mask = jnp.dot(touched, chosen_ref[...], preferred_element_type=f32)
    slot = lax.broadcasted_iota(jnp.int32, (FACETS, DEVICE_SLOTS), 1)
    mask = jnp.where(slot < live_ref[...], mask, 0.0)
    weights = phase_ref[...] * jnp.concatenate([mask, mask], axis=0)
    high, low = split_bf16(weights)
    left = jnp.concatenate(
        [jnp.concatenate([high, high], axis=1), jnp.concatenate([low, jnp.zeros_like(low)], axis=1)],
        axis=0,
    )
    sign = jnp.where(lax.broadcasted_iota(jnp.int32, (FACETS, 2 * S), 1) < S, -1.0, 1.0).astype(f32)

    for l in range(0, S, 2):
        pair = jnp.concatenate(
            [
                towers_ref[l * DEVICE_SLOTS : (l + 1) * DEVICE_SLOTS, :],
                towers_ref[(l + 1) * DEVICE_SLOTS : (l + 2) * DEVICE_SLOTS, :],
            ],
            axis=1,
        )
        high, low = split_bf16(pair)
        sums = jnp.dot(left, jnp.concatenate([high, low], axis=0), preferred_element_type=f32)
        sums = sums[: 2 * FACETS] + sums[2 * FACETS :]
        for k in range(2):
            part = sums[:, 2 * S * k : 2 * S * (k + 1)]
            facet_ref[pl.ds(l + k, FACETS, stride=S), :] = (
                part[:FACETS] + sign * pltpu.roll(part[FACETS:], S, 1)
            )

    shifted = []
    for fy in range(4):
        high, low = split_bf16(facet_ref[4 * S * fy : 4 * S * (fy + 1), :])
        first = jnp.dot(high, right_ref[fy], preferred_element_type=f32)
        second = jnp.dot(low, right_ref[fy, :, : 2 * S], preferred_element_type=f32)
        shifted.append(first[:, : 2 * S] + first[:, 2 * S :] + second)

    wide = jnp.where(lax.broadcasted_iota(jnp.int32, (S, 2 * S), 1) < S, -1.0, 1.0).astype(f32)
    for fx in range(4):
        plain = [rows[S * fx : S * (fx + 1)] for rows in shifted]
        turned = [wide * pltpu.roll(g, S, 1) for g in plain]
        stack = jnp.concatenate(
            [jnp.concatenate(plain, axis=1), jnp.concatenate(turned, axis=1)], axis=0
        )
        high, low = split_bf16(stack)
        shift = left_ref[fx]
        first = jnp.dot(shift, high, preferred_element_type=f32)
        second = jnp.dot(shift[:S], low, preferred_element_type=f32)
        image = first[:S] + first[S:] + second
        for fy in range(4):
            place = (fx + 4 * fy - LINE_Z) % FACETS
            for i in range(2):
                rows_ref[pl.ds(2 * place + i, GROUP, stride=GROUP), :] = image[
                    GROUP * i : GROUP * (i + 1), 2 * S * fy : 2 * S * (fy + 1)
                ]
    out_ref[...] = rows_ref[: FACETS * S].astype(bf16).reshape(GROUP, GROUP, 2 * S)


VMEM = pl.BlockSpec(memory_space=pltpu.VMEM)


def shards(
    visibilities,
    visibility_uv_offsets,
    block_owner_index,
    block_cell_number,
    live_counts,
    touch_lists,
):
    range_index = lax.axis_index("wa")
    touch_group = [((z + TOUCH_Z) % 16) * 4 + (x + TOUCH_X) % 4 for z in range(16) for x in range(4)]
    named = lax.all_to_all(
        jnp.broadcast_to(touch_lists[None].astype(bf16), (N_COL, DEVICE_COLUMNS, TOUCH)),
        ("z", "x"),
        split_axis=0,
        concat_axis=0,
        axis_index_groups=[touch_group],
        tiled=True,
    ).reshape(N_COL * DEVICE_COLUMNS, TOUCH)
    cells = block_cell_number.reshape(1, DEVICE_SLOTS)
    shape = 4 * DEVICE_SLOTS + 8
    half = 2 * DEVICE_SLOTS
    lanes = (0, BLOCK_VISIBILITY - DEVICE_SLOTS)
    packed = (
        jnp.pad(visibilities.reshape(half, BLOCK_VISIBILITY), ((0, shape - half), (0, 0))).astype(f32)
        + jnp.pad(
            visibility_uv_offsets.reshape(half, BLOCK_VISIBILITY), ((half, 8), (0, 0))
        ).astype(f32)
        + jnp.pad(cells, ((2 * half, 7), lanes)).astype(f32)
        + jnp.pad(block_owner_index.reshape(1, DEVICE_SLOTS), ((2 * half + 1, 6), lanes)).astype(f32)
        + jnp.pad(
            range_index.reshape(1, 1).astype(jnp.int32),
            ((2 * half + 2, 5), (0, BLOCK_VISIBILITY - 1)),
        ).astype(f32)
    )
    towers, phases, chosen, left, right = pl.pallas_call(
        grid_kernel,
        out_shape=(
            jax.ShapeDtypeStruct(((S + 1) * DEVICE_SLOTS, 2 * S), f32),
            jax.ShapeDtypeStruct((2 * FACETS, DEVICE_SLOTS), f32),
            jax.ShapeDtypeStruct((DEVICE_COLUMNS * N_COL, DEVICE_SLOTS), bf16),
            jax.ShapeDtypeStruct((4, 2 * S, 2 * S), bf16),
            jax.ShapeDtypeStruct((4, 2 * S, 4 * S), bf16),
        ),
        in_specs=[VMEM],
        out_specs=(VMEM,) * 5,
        scratch_shapes=[
            pltpu.VMEM((8, BLOCK_VISIBILITY), jnp.int32),
            pltpu.SMEM((8, BLOCK_VISIBILITY), jnp.int32),
            pltpu.VMEM((RANGE_PLANES, S, 2 * S), f32),
            pltpu.VMEM((RANGE_PLANES, S, 2 * S), f32),
            pltpu.SemaphoreType.DMA,
        ],
        compiler_params=pltpu.CompilerParams(vmem_limit_bytes=48 * 1024 * 1024),
        cost_estimate=pl.CostEstimate(
            flops=300_000_000, bytes_accessed=2_200_000, transcendentals=0
        ),
        name="grid_blocks",
    )(
        packed,
    )
    partial_rows = pl.pallas_call(
        facet_kernel,
        out_shape=jax.ShapeDtypeStruct((GROUP, GROUP, 2 * S), bf16),
        in_specs=[VMEM] * 7,
        out_specs=VMEM,
        scratch_shapes=[
            pltpu.VMEM((FACETS * S + S, 2 * S), f32),
            pltpu.VMEM((FACETS * S + GROUP, 2 * S), f32),
        ],
        compiler_params=pltpu.CompilerParams(vmem_limit_bytes=24 * 1024 * 1024),
        name="facet_sums",
    )(
        live_counts,
        phases,
        chosen,
        named,
        left,
        right,
        towers,
    )
    arrived = lax.all_to_all(
        partial_rows,
        ("x", "wa"),
        split_axis=0,
        concat_axis=0,
        axis_index_groups=[plane_group()],
        tiled=True,
    )
    plane_rows = jnp.sum(arrived.astype(f32), axis=0)
    arrived = lax.all_to_all(
        plane_rows.reshape(FACETS, 2, 2 * S),
        "z",
        split_axis=0,
        concat_axis=0,
        axis_index_groups=[line_group()],
        tiled=True,
    )
    return jnp.sum(arrived, axis=0)


def solution(mesh):
    grid = Mesh(mesh.devices.reshape(16, 4, N_WA), ("z", "x", "wa"))
    col = ("z", "x")
    placed = (
        P(col, "wa", None, None, None),
        P(col, "wa", None, None, None),
        P(col, "wa", None, None),
        P(col, "wa", None),
        P(col, "wa"),
        P(col, None),
    )
    return jax.shard_map(
        shards, mesh=grid, in_specs=placed, out_specs=P(("z", "x", "wa"), None), check_vma=False
    )
```
